128 devices in a mesh: dp: 2 (over core), seq: 32 (over z, y, x_hi), fsdp: 2 (over x_lo).
Axes of the slice: x: 4 (x_hi: 2, x_lo: 2; x = x_hi * 2 + x_lo), y: 4, z: 4, core: 2. Of those that a mesh axis runs over, the one named last changes fastest.
Arguments:
- activations: bfloat16 [4, 8192, 1536], P(('dp', 'fsdp'), 'seq')
- cotangent: bfloat16 [4, 8192, 1536], P(('dp', 'fsdp'), 'seq'), may hold values from -6 to 6
- lengths: int32 [4], P(('dp', 'fsdp')), may hold values from 2048 to 8192, as said below
- poison: int32 [4, 32], P(('dp', 'fsdp'), 'seq'), may hold values from -1 to 255, as said below
- w_in: bfloat16 [1536, 3072], P('fsdp'), may hold values from -0.15625 to 0.15625
- taps: bfloat16 [1536, 32], P('fsdp'), may hold values from -1.5 to 1.5
Outputs:
- grad_input: bfloat16 [4, 8192, 1536], P(('dp', 'fsdp'), 'seq')
- update_in: float32 [1536, 3072], P(('dp', 'seq', 'fsdp'))
- update_taps: float32 [1536, 32], P(('dp', 'seq', 'fsdp'))
The draws below stay inside these ranges and needn't reach their ends.
Inputs may be any that keep to these rules, and one draw needn't show every extreme that they name: `lengths`: utterance 0 has all 8192 frames valid. `poison`: each utterance has at most one entry other than -1; utterance 0 has none, and utterance 3 has one, at the last frame of its block.
All inputs are finite; a program needn't handle non-finite values.
Results may differ from the reference program's by a relative error of at most 0.01.
Values may be sent and summed in bfloat16 or wider, within the bound.
A program may use at most 128 MiB of HBM per device.

```python
import jax
import jax.numpy as jnp
from jax import lax

D = 1536
KT = 32
ROWS = 256
FRAMES = 8192
BLOCKS = 32
BATCH = 4


def draw_activations(key, part):
    key = jax.random.fold_in(key, 5)
    first, second = jax.random.split(key)
    place = jnp.arange(D, dtype=jnp.float32) / jnp.float32(D)
    jitter = jax.random.uniform(second, (D,), jnp.float32, 0.7, 1.4)
    ramp = jnp.power(jnp.float32(10.0), place)
    base = jnp.clip(jax.random.normal(first, (BATCH, FRAMES, D), jnp.float32), -6.0, 6.0)
    return (base * (ramp * jitter)).astype(jnp.bfloat16)


def draw_lengths(key, part):
    key = jax.random.fold_in(key, 11)
    lens = jax.random.randint(key, (BATCH,), FRAMES // 4, FRAMES + 1).astype(jnp.int32)
    return lens.at[0].set(FRAMES)


def draw_poison(key, part):
    key = jax.random.fold_in(key, 23)
    first, second, third = jax.random.split(key, 3)
    block = jax.random.randint(first, (BATCH,), 0, BLOCKS).astype(jnp.int32)
    offset = jax.random.randint(second, (BATCH,), 0, ROWS).astype(jnp.int32)
    usage = jax.random.randint(third, (BATCH,), 0, 2).astype(jnp.int32)
    usage = usage.at[0].set(0).at[BATCH - 1].set(1)
    offset = offset.at[BATCH - 1].set(ROWS - 1)
    columns = jnp.arange(BLOCKS, dtype=jnp.int32)
    chosen = jnp.logical_and(columns[None, :] == block[:, None], usage[:, None] == 1)
    return jnp.where(chosen, offset[:, None], jnp.int32(-1)).astype(jnp.int32)


def block_scale(rng, extent, shards, smallest, high):
    gain = 1.0
    for position, shards_of in shards:
        heights = jax.random.uniform(jax.random.fold_in(jax.random.fold_in(rng, 6), position), (shards_of,), jnp.float32, smallest / len(shards), high / len(shards))
        gain = gain * jnp.repeat(jnp.exp(heights), extent[position] // shards_of).reshape((-1,) + (1,) * (len(extent) - 1 - position))
    return gain


def scatter_about(own_key, shape, width, most, cuts=(), kind=jnp.bfloat16):
    array = jax.random.normal(own_key, shape, jnp.float32) * width
    if len(cuts) > 0:
        array = block_scale(own_key, shape, cuts, -0.22, 0.18) * array
    return jnp.clip(array, min=-most, max=most).astype(kind)


def setup_inputs(seed: int = 0) -> dict:
    keys = jax.random.split(jax.random.key(seed), 7)
    activations = draw_activations(jax.random.fold_in(keys[6], 71), 0)
    cotangent = scatter_about(keys[1], (BATCH, FRAMES, D), 1.0, 6.0, ((0, 4), (1, 32)))
    lengths = draw_lengths(jax.random.fold_in(keys[6], 71), 0)
    poison = draw_poison(jax.random.fold_in(keys[6], 71), 0)
    w_in = scatter_about(keys[4], (D, 2 * D), D ** -0.5, 0.15625, ((0, 2),))
    taps = scatter_about(keys[5], (D, KT), (KT // 2) ** -0.5, 1.5, ((0, 2),))
    return dict(activations=activations, cotangent=cotangent, lengths=lengths, poison=poison, w_in=w_in, taps=taps)


def normalize_rows(xf):
    row_average = lax.optimization_barrier(jnp.mean(xf, axis=-1, keepdims=True))
    cent = xf - row_average
    var = lax.optimization_barrier(jnp.mean(cent * cent, axis=-1, keepdims=True))
    inverse_deviation = lax.rsqrt(var + 1e-05)
    return (cent * inverse_deviation, inverse_deviation)

def utterance(input_frames, dy, length, bad_cols, w_in, taps):
    half = KT // 2
    frames = jnp.arange(FRAMES, dtype=jnp.int32)
    mask = (frames < length).astype(jnp.float32)[:, None]
    centered_scaled, inverse_deviation = normalize_rows(input_frames.astype(jnp.float32))
    normalized_rows = centered_scaled.astype(jnp.bfloat16)
    pre = jnp.dot(normalized_rows, w_in, preferred_element_type=jnp.float32)
    val = pre[:, :D]
    sig = jax.nn.sigmoid(pre[:, D:])
    glued = (val * sig * mask).astype(jnp.bfloat16)
    gpad = jnp.pad(glued.astype(jnp.float32), ((half, half), (0, 0)))
    tapsf = taps.astype(jnp.float32)
    conv = jnp.zeros((FRAMES, D), jnp.float32)
    for k in range(KT):
        conv = conv + tapsf[:, k] * gpad[k:k + FRAMES]
    swsig = jax.nn.sigmoid(conv)
    starts = jnp.arange(BLOCKS, dtype=jnp.int32) * ROWS + bad_cols
    hit = jnp.any(jnp.logical_and(frames[:, None] == starts[None, :], bad_cols[None, :] >= 0), axis=1)
    seen = jnp.where(hit[:, None], jnp.float32(jnp.inf), dy.astype(jnp.float32))
    row_bad = jnp.any(jnp.logical_not(jnp.isfinite(seen)), axis=1)
    first_bad = jnp.min(jnp.where(row_bad, frames, jnp.int32(FRAMES)))
    cot = jnp.where((frames < first_bad)[:, None], dy, jnp.zeros_like(dy))
    dconv = (cot.astype(jnp.float32) * swsig * (1.0 + conv * (1.0 - swsig))).astype(jnp.bfloat16)
    dcf = dconv.astype(jnp.float32)
    g_taps = jnp.stack([lax.optimization_barrier(jnp.sum(dcf * gpad[k:k + FRAMES], axis=0)) for k in range(KT)], axis=1)
    dpad = jnp.pad(dcf, ((half, half), (0, 0)))
    dglued = jnp.zeros((FRAMES, D), jnp.float32)
    for k in range(KT):
        dglued = dglued + tapsf[:, k] * dpad[2 * half - k:2 * half - k + FRAMES]
    dglued = dglued * mask
    dpre = jnp.concatenate([dglued * sig, dglued * val * sig * (1.0 - sig)], axis=1).astype(jnp.bfloat16)
    g_in = lax.dot_general(normalized_rows, dpre, (((0,), (0,)), ((), ())), preferred_element_type=jnp.float32)
    grad_normalized = lax.dot_general(dpre, w_in, (((1,), (1,)), ((), ())), preferred_element_type=jnp.float32)
    inner_product = grad_normalized - lax.optimization_barrier(jnp.mean(grad_normalized, axis=-1, keepdims=True)) - centered_scaled * lax.optimization_barrier(jnp.mean(grad_normalized * centered_scaled, axis=-1, keepdims=True))
    grad_x = (inverse_deviation * inner_product).astype(jnp.bfloat16)
    return (grad_x, g_in, g_taps)

def reference(activations, cotangent, lengths, poison, w_in, taps):

    def step(carry, items):
        input_frames, dy, length, bad_cols = items
        grad_x, g_in, g_taps = utterance(input_frames, dy, length, bad_cols, w_in, taps)
        return ((carry[0] + g_in, carry[1] + g_taps), grad_x)
    start = (jnp.zeros((D, 2 * D), jnp.float32), jnp.zeros((D, KT), jnp.float32))
    sums, grad_input = lax.scan(step, start, (activations, cotangent, lengths, poison))
    g_in, g_taps = sums
    total = jnp.sum(g_in * g_in) + jnp.sum(g_taps * g_taps)
    msq = total / jnp.float32(2 * D * D + D * KT)
    scale = 1.0 / jnp.maximum(jnp.float32(1.0), jnp.sqrt(msq))
    return (grad_input, g_in * scale, g_taps * scale)
```

```python
import functools

import jax
import jax.numpy as jnp
from jax import lax
from jax.experimental import pallas as pl
from jax.experimental.pallas import tpu as pltpu
from jax.sharding import PartitionSpec as P

MESH = pl.DeviceIdType.MESH
F32 = jnp.float32
BF16 = jnp.bfloat16

D = 1536
H = 768
KT = 32
ROWS = 256
FRAMES = 8192
NC = 6
CH = 128
BIG = FRAMES


def sigmoid(v):
    return 0.5 * jnp.tanh(0.5 * v) + 0.5


def dot(a, b, dims=(((1,), (0,)), ((), ()))):
    return lax.dot_general(a, b, dims, preferred_element_type=F32)


def iota(shape, dim):
    return lax.broadcasted_iota(jnp.int32, shape, dim)


def one_hot(flag):
    return jnp.where(flag, jnp.float32(1.0), jnp.float32(0.0)).astype(BF16)


def await_bytes(ref, sem):
    pltpu.make_async_copy(ref, ref, sem).wait()


def kernel(
    len_ref, poi_ref, taps_ref, x_hbm, cot_hbm, w_hbm,
    gx_ref, gin_ref, gtap_ref,
    x_vm, cot_vm, cot_sib, cot_halo, nn, halo, na, nt, w_vm, cp, cph,
    tap_in, tapf, tb, msk, stat, pre, val_s, sig_s, xe, xh, de, dh, dp, dpn,
    tg, tt, g, r1, s1, r2, fs, r3, sf, t_r1, t_s1, t_r2,
    dno, dns, dnr, fb_s, fb_r, ps_s, ps_r,
    local_sem, w_loc, w_send, w_recv, misc_send, misc_recv, fb_send, fb_recv,
    r1_send, r1_recv, r2_send, r2_recv, r3_send, r3_recv, t_send, t_recv, ps_send, ps_recv,
):
    c = lax.axis_index("dp")
    s = lax.axis_index("seq")
    f = lax.axis_index("fsdp")
    z, y = s // 8, (s // 2) % 4
    x = (s % 2) * 2 + f
    oc = 1 - c

    def dev(core, zz, yy, xx):
        return (core, zz * 8 + yy * 2 + xx // 2, xx % 2)

    def xd(d):
        return (x + d) % 4

    def yd(d):
        return (y + d) % 4

    def zd(d):
        return (z + d) % 4

    nxt, prv = (s + 1) % 32, (s + 31) % 32
    sibling = dev(oc, z, y, x)

    def send(src, dst, send_sem, recv_sem, device):
        pltpu.make_async_remote_copy(
            src_ref=src, dst_ref=dst, send_sem=send_sem, recv_sem=recv_sem,
            device_id=device, device_id_type=MESH,
        ).start()

    partners = [sibling]
    partners += [dev(e, z, y, xd(d)) for d in (1, 2, 3) for e in (0, 1)]
    partners += [dev(c, z, yd(d), x) for d in (1, 2, 3)]
    partners += [dev(c, zd(d), y, x) for d in (1, 2, 3)]
    partners += [(e, q, f) for q in (prv, nxt) for e in (0, 1)]
    barrier = pltpu.get_barrier_semaphore()
    for partner in partners:
        pl.semaphore_signal(barrier, inc=1, device_id=partner, device_id_type=MESH)

    load_x = pltpu.make_async_copy(x_hbm.at[0], x_vm, local_sem.at[0])
    load_cot = pltpu.make_async_copy(cot_hbm.at[0], cot_vm, local_sem.at[1])
    load_cot.start()
    load_x.start()

    def w_columns(j, part):
        return pl.ds(pl.multiple_of(part * D + c * H + j * CH, CH), CH)

    def local_w(j):
        for part in (0, 1):
            pltpu.make_async_copy(
                w_hbm.at[:, w_columns(j, part)],
                w_vm.at[j, pl.ds(pl.multiple_of(f * H, H), H), pl.ds(part * CH, CH)],
                w_loc.at[j],
            ).start()

    def send_w(j):
        for side in (0, 1):
            for part in (0, 1):
                send(
                    w_hbm.at[pl.ds(side * (H // 2), H // 2), w_columns(j, part)],
                    w_vm.at[
                        j,
                        pl.ds(pl.multiple_of(f * H + side * (H // 2), H // 2), H // 2),
                        pl.ds(part * CH, CH),
                    ],
                    w_send.at[j], w_recv.at[j, side], dev(c, z, y, xd(1 if side == 0 else 3)),
                )

    def await_w(j):
        await_bytes(w_vm.at[j, pl.ds(pl.multiple_of(f * H, H), H)], w_loc.at[j])
        for side in (0, 1):
            base = pl.multiple_of((1 - f) * H + side * (H // 2), H // 2)
            await_bytes(w_vm.at[j, pl.ds(base, H // 2)], w_recv.at[j, side])

    for j in range(2):
        local_w(j)

    frame0 = s * ROWS
    load_cot.wait()
    spoiled = jnp.zeros((ROWS, 128), F32)
    for i in range(D // 128):
        spoiled = spoiled + cot_vm[:, i * 128 : (i + 1) * 128].astype(F32) * 0.0
    local = iota((ROWS, 128), 0)
    bad = jnp.logical_or(spoiled != 0.0, local == poi_ref[0, 0])
    cand = jnp.where(bad, frame0 + local, jnp.int32(BIG))
    cand = jnp.min(cand.reshape(ROWS // 8, 8, 128), axis=0)
    cand = jnp.min(jnp.min(cand, axis=0, keepdims=True), axis=1, keepdims=True)
    row = iota((8, 128), 0)
    tile = jnp.where(row == c, jnp.broadcast_to(cand, (8, 128)), jnp.int32(BIG))
    fb_s[0] = jnp.where(row == 2 + c, len_ref[0], tile)

    pl.semaphore_wait(barrier, len(partners))

    send_w(0)
    for k, partner in enumerate((sibling, dev(c, z, y, xd(2)), dev(oc, z, y, xd(2)))):
        send(fb_s.at[0], fb_r.at[0, k], fb_send.at[0], fb_recv.at[0], partner)
    send(
        cot_vm.at[:, pl.ds(pl.multiple_of(oc * H, H), H)], cot_sib,
        misc_send.at[0], misc_recv.at[0], sibling,
    )
    for e in (0, 1):
        cols = pl.ds(e * H, H)
        send(cot_vm.at[pl.ds(ROWS - 16, 16), cols], cot_halo.at[c, 0],
             misc_send.at[1], misc_recv.at[1], (e, nxt, f))
        send(cot_vm.at[pl.ds(0, 16), cols], cot_halo.at[c, 1],
             misc_send.at[1], misc_recv.at[1], (e, prv, f))
    send(taps_ref, tap_in, misc_send.at[2], misc_recv.at[2], dev(c, z, y, xd(3)))
    send_w(1)

    load_x.wait()

    def norm_rows(i, _):
        rows = pl.ds(pl.multiple_of(i * 32, 32), 32)
        xf = x_vm[rows, :].astype(F32)
        average = jnp.mean(xf, axis=-1, keepdims=True)
        cent = xf - average
        inverse = lax.rsqrt(jnp.mean(cent * cent, axis=-1, keepdims=True) + 1e-05)
        nn[rows, :] = (cent * inverse).astype(BF16)
        stat[0, rows, :] = jnp.broadcast_to(average, (32, 128))
        stat[1, rows, :] = jnp.broadcast_to(inverse, (32, 128))
        return 0

    lax.fori_loop(0, ROWS // 32, norm_rows, 0)
    send(nn.at[pl.ds(ROWS - 32, 32)], halo.at[c, 0], misc_send.at[3], misc_recv.at[3], (c, nxt, f))
    send(nn.at[pl.ds(0, 32)], halo.at[c, 1], misc_send.at[3], misc_recv.at[3], (c, prv, f))

    r0, r1i = iota((ROWS, ROWS), 0), iota((ROWS, ROWS), 1)
    to_phase = one_hot((r0 % 8) * 32 + r0 // 8 == r1i)
    own_rows = pl.ds(pl.multiple_of(c * ROWS, ROWS), ROWS)
    sib_rows = pl.ds(pl.multiple_of(oc * ROWS, ROWS), ROWS)
    na[own_rows, :] = dot(to_phase, nn[...]).astype(BF16)
    send(na.at[own_rows], na.at[own_rows], misc_send.at[4], misc_recv.at[4], sibling)

    await_bytes(fb_r.at[0], fb_recv.at[0])
    fb_s[1] = jnp.minimum(jnp.minimum(fb_s[0], fb_r[0, 0]), jnp.minimum(fb_r[0, 1], fb_r[0, 2]))
    for d in (1, 2, 3):
        send(fb_s.at[1], fb_r.at[1, d - 1], fb_send.at[1], fb_recv.at[1], dev(c, z, yd(d), x))

    for i in range(D // 128):
        cols = pl.ds(i * 128, 128)
        nt[cols, own_rows] = na[own_rows, cols].T

    await_bytes(halo.at[c], misc_recv.at[3])
    send(halo.at[c], halo.at[c], misc_send.at[5], misc_recv.at[5], sibling)

    await_bytes(fb_r.at[1], fb_recv.at[1])
    fb_s[2] = jnp.minimum(jnp.minimum(fb_s[1], fb_r[1, 0]), jnp.minimum(fb_r[1, 1], fb_r[1, 2]))
    for d in (1, 2, 3):
        send(fb_s.at[2], fb_r.at[2, d - 1], fb_send.at[2], fb_recv.at[2], dev(c, zd(d), y, x))

    await_bytes(tap_in, misc_recv.at[2])
    mine = jnp.where(f == c, jnp.float32(1.0), jnp.float32(0.0))
    tapf[...] = taps_ref[...].astype(F32) * mine + tap_in[...].astype(F32) * (1.0 - mine)

    await_bytes(na.at[sib_rows], misc_recv.at[4])
    for i in range(D // 128):
        cols = pl.ds(i * 128, 128)
        nt[cols, sib_rows] = na[sib_rows, cols].T
    await_bytes(halo.at[oc], misc_recv.at[5])
    h0, h1 = iota((128, 128), 0), iota((128, 128), 1)
    source = ((h0 % 4) * 32) + ((h0 // 4) % 2) * 16 + h0 // 8
    halo_order = one_hot(source == h1)
    na[512:640, :] = dot(halo_order, halo[...].reshape(128, D)).astype(BF16)

    await_bytes(fb_r.at[2], fb_recv.at[2])
    votes = jnp.minimum(jnp.minimum(fb_s[2], fb_r[2, 0]), jnp.minimum(fb_r[2, 1], fb_r[2, 2]))
    await_bytes(cot_sib, misc_recv.at[0])
    await_bytes(cot_halo, misc_recv.at[1])
    ra = iota((ROWS, 128), 0)
    frame = frame0 + (ra % 8) * 32 + ra // 8
    for own in (True, False):
        if own:
            part = cot_vm[:, pl.ds(pl.multiple_of(c * H, H), H)]
            u = c
        else:
            part = cot_sib[...]
            u = oc
        first = jnp.min(
            jnp.where(iota((8, 128), 0) == u, votes, jnp.int32(BIG)), axis=0, keepdims=True
        )
        keep = jnp.where(frame < first, jnp.float32(1.0), jnp.float32(0.0))
        moved = dot(to_phase, part)
        for i in range(NC):
            cp[u, :, i * CH : (i + 1) * CH] = (moved[:, i * CH : (i + 1) * CH] * keep).astype(BF16)
    c0, c1 = iota((128, 64), 0), iota((128, 64), 1)
    edge_order = one_hot(
        jnp.logical_and(c0 % 8 < 4, (c0 % 8) * 16 + c0 // 8 == c1)
    )
    hr = iota((128, 128), 0)
    place, q = hr % 8, hr // 8
    edge_frame = frame0 + jnp.where(place % 2 == 0, q - 16, q + ROWS)
    limit = jnp.where((place // 2) % 2 == 0, votes[0:1], votes[1:2])
    keep = jnp.logical_and(edge_frame >= 0, edge_frame < limit)
    keep = jnp.where(keep, jnp.float32(1.0), jnp.float32(0.0))
    moved = dot(edge_order, cot_halo[...].reshape(64, H))
    for i in range(NC):
        cph[:, i * CH : (i + 1) * CH] = (moved[:, i * CH : (i + 1) * CH] * keep).astype(BF16)

    for u in (0, 1):
        msk[u * ROWS : (u + 1) * ROWS, :] = jnp.where(
            frame < votes[2 + u : 3 + u], jnp.float32(1.0), jnp.float32(0.0)
        )
    halo_frame = frame0 + jnp.where(place % 2 == 0, q - 32, q + ROWS) + (place // 4) * 16
    limit = jnp.where((place // 2) % 2 == 0, votes[2:3], votes[3:4])
    keep = jnp.logical_and(halo_frame >= 0, halo_frame < limit)
    msk[512:640, :] = jnp.where(keep, jnp.float32(1.0), jnp.float32(0.0))

    from_phase = one_hot((r1i % 8) * 32 + r1i // 8 == r0)

    def stage1_start(j):
        for d in (1, 2, 3):
            send(g.at[j, 0, :, zd(d)], r1.at[j, 0, d - 1], r1_send.at[j, 0], r1_recv.at[j, 0],
                 dev(c, zd(d), y, x))
            send(g.at[j, 1, :, :, yd(d)], r1.at[j, 1, d - 1], r1_send.at[j, 1], r1_recv.at[j, 1],
                 dev(c, z, yd(d), x))

    def stage1_finish(j):
        for part in (0, 1):
            await_bytes(r1.at[j, part], r1_recv.at[j, part])

            def add(i, _):
                a, b = i // 4, i % 4
                mine = g[j, 0, a, z, b] if part == 0 else g[j, 1, a, b, y]
                total = mine.astype(F32)
                for d in range(3):
                    total = total + r1[j, part, d, a, b].astype(F32)
                s1[j, part, a, b] = total.astype(BF16)
                return 0

            lax.fori_loop(0, 8, add, 0)
        for d in (1, 2, 3):
            send(s1.at[j, 0, :, yd(d)], r2.at[j, 0, d - 1], r2_send.at[j, 0], r2_recv.at[j, 0],
                 dev(c, z, yd(d), x))
            send(s1.at[j, 1, :, zd(d)], r2.at[j, 1, d - 1], r2_send.at[j, 1], r2_recv.at[j, 1],
                 dev(c, zd(d), y, x))

    def stage2_finish(j):
        for part in (0, 1):
            await_bytes(r2.at[j, part], r2_recv.at[j, part])
            lanes = pl.ds(pl.multiple_of(j * 256 + part * 128, 128), 128)
            for a in (0, 1):
                total = s1[j, part, a, y if part == 0 else z].astype(F32)
                for d in range(3):
                    total = total + r2[j, part, d, a].astype(F32)
                sf[a, 0:48] = total
                for b in range(4):
                    fs[a, b, :, lanes] = sf[a, 12 * b : 12 * b + 16].astype(BF16)

    sf[...] = jnp.zeros_like(sf)
    tg[...] = jnp.zeros_like(tg)
    for a in (0, 1):
        for b in range(4):
            fs[a, b, :, 1536:1664] = jnp.zeros((16, 128), BF16)

    sub = iota((16, 8, 128), 1)

    def chunk(j, _):
        @pl.when(j + 2 < NC)
        def _():
            local_w(j + 2)
            send_w(j + 2)

        lanes = pl.ds(pl.multiple_of(j * CH, CH), CH)
        for k in range(KT):
            tb[k] = jnp.broadcast_to(tapf[k : k + 1, lanes], (8, 128))
        await_w(j)
        pre[...] = dot(na[...], w_vm[j])

        def gated(rows):
            sig = sigmoid(pre[rows, CH:])
            val = pre[rows, :CH]
            return val, sig, val * sig * msk[rows, :]

        main = []
        for u in (0, 1):
            rows = slice(u * ROWS, (u + 1) * ROWS)
            val, sig, glued = gated(rows)
            val_s[rows, :] = val
            sig_s[rows, :] = sig
            xe[u, 16:48] = glued.reshape(32, 8, CH)
        h3 = gated(slice(512, 640))[2].reshape(16, 8, CH)
        h4 = pltpu.roll(h3, 4, 1)
        for u in (0, 1):
            left = h4 if u == 0 else pltpu.roll(h3, 2, 1)
            xe[u, 0:16] = jnp.where(sub == 0, left, pltpu.roll(xe[u, 32:48], 1, 1))
            xe[u, 48:64] = jnp.where(
                sub == 7, pltpu.roll(h3, 6 - 2 * u, 1), pltpu.roll(xe[u, 16:32], 7, 1)
            )
        xh[0:16] = jnp.where(
            sub == 1, pltpu.roll(xe[0, 32:48], 2, 1),
            jnp.where(sub == 3, pltpu.roll(xe[1, 32:48], 4, 1), h3),
        )
        xh[16:32] = jnp.where(sub % 2 == 0, h4, h3)
        xh[32:48] = jnp.where(
            sub == 0, xe[0, 16:32], jnp.where(sub == 2, pltpu.roll(xe[1, 16:32], 2, 1), h4)
        )

        def conv(window):
            total = tb[0][None] * window[0:8]
            for k in range(1, KT):
                total = total + tb[k][None] * window[k : k + 8]
            return total

        def through_swish(total, cot):
            gate = sigmoid(total)
            return cot * gate * (1.0 + total * (1.0 - gate))

        def forward(i, _):
            u, b = i // 4, i % 4
            total = conv(xe[u, pl.ds(b * 8, 39)])
            cot = cp[u, pl.ds(pl.multiple_of(b * 64, 64), 64), lanes].astype(F32)
            de[u, pl.ds(16 + b * 8, 8)] = through_swish(total, cot.reshape(8, 8, CH))
            return 0

        lax.fori_loop(0, 8, forward, 0)

        def forward_edge(b, _):
            total = conv(xh[pl.ds(b * 8, 39)])
            cot = cph[pl.ds(pl.multiple_of(b * 64, 64), 64), lanes].astype(F32)
            dh[pl.ds(b * 8, 8)] = through_swish(total, cot.reshape(8, 8, CH))
            return 0

        lax.fori_loop(0, 2, forward_edge, 0)
        d3 = dh[...]
        for u in (0, 1):
            left = d3 if u == 0 else pltpu.roll(d3, 6, 1)
            de[u, 0:16] = jnp.where(sub == 0, left, pltpu.roll(de[u, 32:48], 1, 1))
            de[u, 48:64] = jnp.where(
                sub == 7, pltpu.roll(d3, 6 - 2 * u, 1), pltpu.roll(de[u, 16:32], 7, 1)
            )

        def backward(i, _):
            u, b = i // 4, i % 4
            window = de[u, pl.ds(b * 8 + 1, 39)]
            total = tb[0][None] * window[31:39]
            for k in range(1, KT):
                total = total + tb[k][None] * window[31 - k : 39 - k]
            rows = pl.ds(pl.multiple_of(i * 64, 64), 64)
            dglued = total.reshape(64, CH) * msk[rows, :]
            val, sig = val_s[rows, :], sig_s[rows, :]
            dval = dglued * sig
            dp[rows, 0:CH] = dval.astype(BF16)
            dp[rows, CH:] = (dval * val * (1.0 - sig)).astype(BF16)
            return 0

        lax.fori_loop(0, 8, backward, 0)

        def tap_terms(i, total):
            u, b = i // 4, i % 4
            window = xe[u, pl.ds(b * 8, 39)]
            grads = de[u, pl.ds(16 + b * 8, 8)]
            for m in range(8):
                total = total + grads[m][None] * window[m : m + 32]
            return total

        terms = lax.fori_loop(0, 8, tap_terms, jnp.zeros((KT, 8, CH), F32))
        tg[j, 0:KT] = jnp.sum(terms, axis=1)

        for i in range(8):
            grad = dot(nt[i * 192 : (i + 1) * 192, :], dp[...])
            for part in (0, 1):
                half = grad[:, part * CH : (part + 1) * CH].astype(BF16)
                g[j, part, i // 4, i % 4] = half.reshape(4, 48, CH)
        stage1_start(j)
        for u in (0, 1):
            rows = slice(u * ROWS, (u + 1) * ROWS)
            dpn[j, rows, :] = dot(from_phase, dp[rows, :]).astype(BF16)

        @pl.when(j >= 1)
        def _():
            stage1_finish(j - 1)

        @pl.when(j >= 2)
        def _():
            stage2_finish(j - 2)

        return 0

    lax.fori_loop(0, NC, chunk, 0)

    for j in range(NC):
        tt[j * CH : (j + 1) * CH, :] = tg[j].T.astype(BF16)
    for d in (1, 2, 3):
        send(tt.at[pl.ds(pl.multiple_of(zd(d) * 192, 16), 192)], t_r1.at[d - 1],
             t_send.at[0], t_recv.at[0], dev(c, zd(d), y, x))

    dims = (((1,), (1,)), ((), ()))

    def dnormed(u, cols):
        rows = pl.ds(pl.multiple_of(u * ROWS, ROWS), ROWS)
        total = dot(dpn[0, rows, :], w_vm[0, cols, :], dims)
        for j in range(1, NC):
            total = total + dot(dpn[j, rows, :], w_vm[j, cols, :], dims)
        return total

    def sibling_part(i, _):
        cols = pl.ds(pl.multiple_of(i * 256, 256), 256)
        dns[:, cols] = dnormed(oc, cols).astype(BF16)
        return 0

    lax.fori_loop(0, D // 256, sibling_part, 0)
    send(dns, dnr, misc_send.at[6], misc_recv.at[6], sibling)

    stage1_finish(NC - 1)
    stage2_finish(NC - 2)
    await_bytes(t_r1, t_recv.at[0])
    mine = tt[pl.ds(pl.multiple_of(z * 192, 16), 192), :].astype(F32)
    for d in range(3):
        mine = mine + t_r1[d].astype(F32)
    t_s1[...] = mine.astype(BF16)
    for d in (1, 2, 3):
        send(t_s1.at[pl.ds(pl.multiple_of(yd(d) * 48, 16), 48)], t_r2.at[d - 1],
             t_send.at[1], t_recv.at[1], dev(c, z, yd(d), x))

    def own_part(i, _):
        cols = pl.ds(pl.multiple_of(i * 256, 256), 256)
        dno[:, cols] = dnormed(c, cols)
        return 0

    lax.fori_loop(0, D // 256, own_part, 0)

    stage2_finish(NC - 1)
    await_bytes(t_r2, t_recv.at[1])
    mine = t_s1[pl.ds(pl.multiple_of(y * 48, 16), 48), :].astype(F32)
    for d in range(3):
        mine = mine + t_r2[d].astype(F32)
    sf[0, 0:48] = mine
    for b in range(4):
        fs[c, b, :, 1536:1664] = sf[0, 12 * b : 12 * b + 16].astype(BF16)

    for e in (0, 1):
        core = c if e == 0 else oc
        for d in range(4):
            if e == 0 and d == 0:
                continue
            send(fs.at[core, xd(d)], r3.at[e, d], r3_send.at[e], r3_recv.at[e],
                 dev(core, z, y, xd(d)))

    await_bytes(dnr, misc_recv.at[6])

    def input_rows(i, _):
        rows = pl.ds(pl.multiple_of(i * 32, 32), 32)
        average, inverse = stat[0, rows, 0:1], stat[1, rows, 0:1]
        xhat = (x_vm[rows, :].astype(F32) - average) * inverse
        grad = dno[rows, :] + dnr[rows, :].astype(F32)
        m1 = jnp.mean(grad, axis=-1, keepdims=True)
        m2 = jnp.mean(grad * xhat, axis=-1, keepdims=True)
        gx_ref[0, rows, :] = (inverse * (grad - m1 - xhat * m2)).astype(BF16)
        return 0

    lax.fori_loop(0, ROWS // 32, input_rows, 0)

    await_bytes(r3.at[0, 1:4], r3_recv.at[0])
    await_bytes(r3.at[1], r3_recv.at[1])
    r3[0, 0] = fs[c, x]
    squares = jnp.zeros((12, 128), F32)
    for e in (0, 1):
        core = c if e == 0 else oc
        for i in range(2 * NC):
            total = r3[e, 0, :, i * 128 : (i + 1) * 128].astype(F32)
            for d in range(1, 4):
                total = total + r3[e, d, :, i * 128 : (i + 1) * 128].astype(F32)
            total = total[0:12]
            squares = squares + total * total
            at = pl.multiple_of((i % 2) * D + core * H + (i // 2) * CH, CH)
            gin_ref[:, pl.ds(at, CH)] = total
    total = r3[0, 0, :, 1536:1664].astype(F32)
    for d in range(1, 4):
        total = total + r3[0, d, :, 1536:1664].astype(F32)
    tap_rows = total[0:12]
    squares = squares + tap_rows * tap_rows

    part = jnp.sum(jnp.sum(squares, axis=0, keepdims=True), axis=1, keepdims=True)
    ps_s[0] = jnp.broadcast_to(part, (8, 128))
    count = 0
    for e in (0, 1):
        for d in range(4):
            if e == 0 and d == 0:
                continue
            send(ps_s.at[0], ps_r.at[count], ps_send.at[0], ps_recv.at[0],
                 dev(c if e == 0 else oc, z, y, xd(d)))
            count += 1
    await_bytes(ps_r.at[0:7], ps_recv.at[0])
    total = ps_s[0]
    for i in range(7):
        total = total + ps_r[i]
    ps_s[1] = total
    for d in (1, 2, 3):
        send(ps_s.at[1], ps_r.at[6 + d], ps_send.at[1], ps_recv.at[1], dev(c, z, yd(d), x))
    await_bytes(ps_r.at[7:10], ps_recv.at[1])
    total = ps_s[1] + ps_r[7] + ps_r[8] + ps_r[9]
    ps_s[2] = total
    for d in (1, 2, 3):
        send(ps_s.at[2], ps_r.at[9 + d], ps_send.at[2], ps_recv.at[2], dev(c, zd(d), y, x))
    await_bytes(ps_r.at[10:13], ps_recv.at[2])
    total = ps_s[2] + ps_r[10] + ps_r[11] + ps_r[12]
    msq = total[0:1, 0:1] / jnp.float32(2 * D * D + D * KT)
    scale = 1.0 / jnp.maximum(jnp.float32(1.0), jnp.sqrt(msq))
    gin_ref[...] = gin_ref[...] * scale
    gtap_ref[...] = (tap_rows * scale)[:, 0:KT]

    for j in range(NC):
        await_bytes(w_vm.at[j, pl.ds(0, H)], w_send.at[j])
        for part in (0, 1):
            await_bytes(r1.at[j, part], r1_send.at[j, part])
            await_bytes(r2.at[j, part], r2_send.at[j, part])
    await_bytes(cot_sib, misc_send.at[0])
    await_bytes(cot_halo, misc_send.at[1])
    await_bytes(tap_in, misc_send.at[2])
    await_bytes(halo.at[c], misc_send.at[3])
    await_bytes(na.at[own_rows], misc_send.at[4])
    await_bytes(halo.at[c], misc_send.at[5])
    await_bytes(dns, misc_send.at[6])
    for i in range(3):
        await_bytes(fb_r.at[i], fb_send.at[i])
    await_bytes(r3.at[0, 1:4], r3_send.at[0])
    await_bytes(r3.at[1], r3_send.at[1])
    await_bytes(t_r1, t_send.at[0])
    await_bytes(t_r2, t_send.at[1])
    await_bytes(ps_r.at[0:7], ps_send.at[0])
    await_bytes(ps_r.at[7:10], ps_send.at[1])
    await_bytes(ps_r.at[10:13], ps_send.at[2])


def body(activations, cotangent, lengths, poison, w_in, taps):
    vmem = pltpu.VMEM
    dma = pltpu.SemaphoreType.DMA
    scratch = [
        vmem((ROWS, D), BF16),
        vmem((ROWS, D), BF16),
        vmem((ROWS, H), BF16),
        vmem((2, 2, 16, H), BF16),
        vmem((ROWS, D), BF16),
        vmem((2, 2, 32, D), BF16),
        vmem((640, D), BF16),
        vmem((D, 512), BF16),
        vmem((NC, D, 2 * CH), BF16),
        vmem((2, ROWS, H), BF16),
        vmem((128, H), BF16),
        vmem((KT, H), BF16),
        vmem((KT, H), F32),
        vmem((KT, 8, CH), F32),
        vmem((640, 128), F32),
        vmem((2, ROWS, 128), F32),
        vmem((640, 2 * CH), F32),
        vmem((512, CH), F32),
        vmem((512, CH), F32),
        vmem((2, 64, 8, CH), F32),
        vmem((48, 8, CH), F32),
        vmem((2, 64, 8, CH), F32),
        vmem((16, 8, CH), F32),
        vmem((512, 2 * CH), BF16),
        vmem((NC, 512, 2 * CH), BF16),
        vmem((NC, 128, CH), F32),
        vmem((H, 128), BF16),
        vmem((NC, 2, 2, 4, 4, 48, CH), BF16),
        vmem((NC, 2, 3, 2, 4, 48, CH), BF16),
        vmem((NC, 2, 2, 4, 48, CH), BF16),
        vmem((NC, 2, 3, 2, 48, CH), BF16),
        vmem((2, 4, 16, 1664), BF16),
        vmem((2, 4, 16, 1664), BF16),
        vmem((2, 56, CH), F32),
        vmem((3, 192, 128), BF16),
        vmem((192, 128), BF16),
        vmem((3, 48, 128), BF16),
        vmem((ROWS, D), F32),
        vmem((ROWS, D), BF16),
        vmem((ROWS, D), BF16),
        vmem((3, 8, 128), jnp.int32),
        vmem((3, 3, 8, 128), jnp.int32),
        vmem((3, 8, 128), F32),
        vmem((13, 8, 128), F32),
        dma((2,)),
        dma((NC,)), dma((NC,)), dma((NC, 2)),
        dma((7,)), dma((7,)),
        dma((3,)), dma((3,)),
        dma((NC, 2)), dma((NC, 2)),
        dma((NC, 2)), dma((NC, 2)),
        dma((2,)), dma((2,)),
        dma((2,)), dma((2,)),
        dma((3,)), dma((3,)),
    ]
    anywhere = pl.BlockSpec(memory_space=pl.ANY)
    in_vmem = pl.BlockSpec(memory_space=pltpu.VMEM)
    in_smem = pl.BlockSpec(memory_space=pltpu.SMEM)
    return pl.pallas_call(
        kernel,
        out_shape=(
            jax.ShapeDtypeStruct((1, ROWS, D), BF16),
            jax.ShapeDtypeStruct((12, 2 * D), F32),
            jax.ShapeDtypeStruct((12, KT), F32),
        ),
        in_specs=[in_smem, in_smem, in_vmem, anywhere, anywhere, anywhere],
        out_specs=(in_vmem, in_vmem, in_vmem),
        scratch_shapes=scratch,
        compiler_params=pltpu.CompilerParams(
            collective_id=0, has_side_effects=True, vmem_limit_bytes=56 * 1024 * 1024
        ),
        name="conformer_conv",
    )(lengths, poison, taps.T, activations, cotangent, w_in)


def solution(mesh):
    placed = (
        P(("dp", "fsdp"), "seq", None),
        P(("dp", "fsdp"), "seq", None),
        P(("dp", "fsdp")),
        P(("dp", "fsdp"), "seq"),
        P("fsdp", None),
        P("fsdp", None),
    )
    return jax.shard_map(
        body,
        mesh=mesh,
        in_specs=placed,
        out_specs=(
            P(("dp", "fsdp"), "seq", None),
            P(("dp", "seq", "fsdp"), None),
            P(("dp", "seq", "fsdp"), None),
        ),
        check_vma=False,
    )
```

```python
import functools

import jax
import jax.numpy as jnp
from jax import lax
from jax.experimental import pallas as pl
from jax.experimental.pallas import tpu as pltpu
from jax.sharding import PartitionSpec as P

MESH = pl.DeviceIdType.MESH
F32 = jnp.float32
BF16 = jnp.bfloat16

D = 1536
H = 768
KT = 32
ROWS = 256
FRAMES = 8192
NC = 6
CH = 128
BIG = FRAMES


def sigmoid(v):
    return 0.5 * jnp.tanh(0.5 * v) + 0.5


def dot(a, b, dims=(((1,), (0,)), ((), ()))):
    return lax.dot_general(a, b, dims, preferred_element_type=F32)


def iota(shape, dim):
    return lax.broadcasted_iota(jnp.int32, shape, dim)


def one_hot(flag):
    return jnp.where(flag, jnp.float32(1.0), jnp.float32(0.0)).astype(BF16)


def await_bytes(ref, sem):
    pltpu.make_async_copy(ref, ref, sem).wait()


def kernel(
    len_ref, poi_ref, taps_ref, x_hbm, cot_hbm, w_hbm,
    gx_hbm, gin_hbm, gtap_hbm,
    x_vm, cot_vm, cot_sib, cot_halo, edges, nn, halo, na, nt, w_vm, cp, cph,
    tap_in, tapf, tb, msk, keep, stat, pre, val_s, sig_s, xe, xh, de, dh, dp, dpn,
    tg, tt, g, r1, s1, r2, fs, r3, sf, t_r1, t_s1, t_r2,
    dno, dns, dnr, gx_vm, gin_vm, gtap_vm, fb_s, fb_r, ps_s, ps_r,
    local_sem, w_loc, w_send, w_recv, misc_send, misc_recv, fb_send, fb_recv,
    r1_send, r1_recv, r2_send, r2_recv, r3_send, r3_recv, t_send, t_recv, ps_send, ps_recv,
):
    c = lax.axis_index("dp")
    s = lax.axis_index("seq")
    f = lax.axis_index("fsdp")
    z, y = s // 8, (s // 2) % 4
    x = (s % 2) * 2 + f
    oc = 1 - c

    def dev(core, zz, yy, xx):
        return (core, zz * 8 + yy * 2 + xx // 2, xx % 2)

    def xd(d):
        return (x + d) % 4

    def yd(d):
        return (y + d) % 4

    def zd(d):
        return (z + d) % 4

    nxt, prv = (s + 1) % 32, (s + 31) % 32
    sibling = dev(oc, z, y, x)

    def send(src, dst, send_sem, recv_sem, device):
        pltpu.make_async_remote_copy(
            src_ref=src, dst_ref=dst, send_sem=send_sem, recv_sem=recv_sem,
            device_id=device, device_id_type=MESH,
        ).start()

    partners = [sibling]
    partners += [dev(e, z, y, xd(d)) for d in (1, 2, 3) for e in (0, 1)]
    partners += [dev(c, z, yd(d), x) for d in (1, 2, 3)]
    partners += [dev(c, zd(d), y, x) for d in (1, 2, 3)]
    partners += [(e, q, f) for q in (prv, nxt) for e in (0, 1)]
    barrier = pltpu.get_barrier_semaphore()
    for partner in partners:
        pl.semaphore_signal(barrier, inc=1, device_id=partner, device_id_type=MESH)

    load_x = pltpu.make_async_copy(x_hbm.at[0], x_vm, local_sem.at[0])
    load_cot = pltpu.make_async_copy(cot_hbm.at[0], cot_vm, local_sem.at[1])
    load_cot.start()
    load_x.start()

    def w_columns(j, part):
        return pl.ds(pl.multiple_of(part * D + c * H + j * CH, CH), CH)

    def local_w(j):
        for part in (0, 1):
            pltpu.make_async_copy(
                w_hbm.at[:, w_columns(j, part)],
                w_vm.at[j, pl.ds(pl.multiple_of(f * H, H), H), pl.ds(part * CH, CH)],
                w_loc.at[j],
            ).start()

    def send_w(j):
        for side in (0, 1):
            for part in (0, 1):
                send(
                    w_hbm.at[pl.ds(side * (H // 2), H // 2), w_columns(j, part)],
                    w_vm.at[
                        j,
                        pl.ds(pl.multiple_of(f * H + side * (H // 2), H // 2), H // 2),
                        pl.ds(part * CH, CH),
                    ],
                    w_send.at[j], w_recv.at[j, side], dev(c, z, y, xd(1 if side == 0 else 3)),
                )

    def await_w(j):
        await_bytes(w_vm.at[j, pl.ds(pl.multiple_of(f * H, H), H)], w_loc.at[j])
        for side in (0, 1):
            base = pl.multiple_of((1 - f) * H + side * (H // 2), H // 2)
            await_bytes(w_vm.at[j, pl.ds(base, H // 2)], w_recv.at[j, side])

    for j in range(NC):
        local_w(j)

    frame0 = s * ROWS
    load_cot.wait()
    spoiled = jnp.zeros((ROWS, 128), F32)
    for i in range(D // 128):
        spoiled = spoiled + cot_vm[:, i * 128 : (i + 1) * 128].astype(F32) * 0.0
    local = iota((ROWS, 128), 0)
    bad = jnp.logical_or(spoiled != 0.0, local == poi_ref[0, 0])
    cand = jnp.where(bad, frame0 + local, jnp.int32(BIG))
    cand = jnp.min(cand.reshape(ROWS // 8, 8, 128), axis=0)
    cand = jnp.min(jnp.min(cand, axis=0, keepdims=True), axis=1, keepdims=True)
    row = iota((8, 128), 0)
    tile = jnp.where(row == c, jnp.broadcast_to(cand, (8, 128)), jnp.int32(BIG))
    fb_s[0] = jnp.where(row == 2 + c, len_ref[0], tile)

    pl.semaphore_wait(barrier, len(partners))

    send(x_hbm.at[0, pl.ds(ROWS - 32, 32)], edges.at[0], misc_send.at[3], misc_recv.at[3], (c, nxt, f))
    send(x_hbm.at[0, pl.ds(0, 32)], edges.at[1], misc_send.at[3], misc_recv.at[3], (c, prv, f))
    for k, partner in enumerate((sibling, dev(c, z, y, xd(2)), dev(oc, z, y, xd(2)))):
        send(fb_s.at[0], fb_r.at[0, k], fb_send.at[0], fb_recv.at[0], partner)
    send(
        cot_vm.at[:, pl.ds(pl.multiple_of(oc * H, H), H)], cot_sib,
        misc_send.at[0], misc_recv.at[0], sibling,
    )
    for e in (0, 1):
        cols = pl.ds(e * H, H)
        send(cot_vm.at[pl.ds(ROWS - 16, 16), cols], cot_halo.at[c, 0],
             misc_send.at[1], misc_recv.at[1], (e, nxt, f))
        send(cot_vm.at[pl.ds(0, 16), cols], cot_halo.at[c, 1],
             misc_send.at[1], misc_recv.at[1], (e, prv, f))
    send(taps_ref, tap_in, misc_send.at[2], misc_recv.at[2], dev(c, z, y, xd(3)))
    for j in range(NC):
        send_w(j)

    load_x.wait()

    def normalised(frames):
        xf = frames.astype(F32)
        average = jnp.mean(xf, axis=-1, keepdims=True)
        cent = xf - average
        inverse = lax.rsqrt(jnp.mean(cent * cent, axis=-1, keepdims=True) + 1e-05)
        return (cent * inverse).astype(BF16), average, inverse

    def norm_rows(i, _):
        rows = pl.ds(pl.multiple_of(i * 32, 32), 32)
        nn[rows, :], average, inverse = normalised(x_vm[rows, :])
        stat[0, rows, :] = jnp.broadcast_to(average, (32, 128))
        stat[1, rows, :] = jnp.broadcast_to(inverse, (32, 128))
        return 0

    lax.fori_loop(0, ROWS // 32, norm_rows, 0)

    r0, r1i = iota((ROWS, ROWS), 0), iota((ROWS, ROWS), 1)
    to_phase = one_hot((r0 % 8) * 32 + r0 // 8 == r1i)
    own_rows = pl.ds(pl.multiple_of(c * ROWS, ROWS), ROWS)
    sib_rows = pl.ds(pl.multiple_of(oc * ROWS, ROWS), ROWS)
    na[own_rows, :] = dot(to_phase, nn[...]).astype(BF16)
    send(na.at[own_rows], na.at[own_rows], misc_send.at[4], misc_recv.at[4], sibling)

    await_bytes(fb_r.at[0], fb_recv.at[0])
    fb_s[1] = jnp.minimum(jnp.minimum(fb_s[0], fb_r[0, 0]), jnp.minimum(fb_r[0, 1], fb_r[0, 2]))
    for d in (1, 2, 3):
        send(fb_s.at[1], fb_r.at[1, d - 1], fb_send.at[1], fb_recv.at[1], dev(c, z, yd(d), x))

    for i in range(D // 128):
        cols = pl.ds(i * 128, 128)
        nt[cols, own_rows] = na[own_rows, cols].T

    await_bytes(edges, misc_recv.at[3])
    for side in (0, 1):
        halo[c, side] = normalised(edges[side])[0]
    send(halo.at[c], halo.at[c], misc_send.at[5], misc_recv.at[5], sibling)

    await_bytes(fb_r.at[1], fb_recv.at[1])
    fb_s[2] = jnp.minimum(jnp.minimum(fb_s[1], fb_r[1, 0]), jnp.minimum(fb_r[1, 1], fb_r[1, 2]))
    for d in (1, 2, 3):
        send(fb_s.at[2], fb_r.at[2, d - 1], fb_send.at[2], fb_recv.at[2], dev(c, zd(d), y, x))

    await_bytes(tap_in, misc_recv.at[2])
    mine = jnp.where(f == c, jnp.float32(1.0), jnp.float32(0.0))
    tapf[...] = taps_ref[...].astype(F32) * mine + tap_in[...].astype(F32) * (1.0 - mine)

    await_bytes(na.at[sib_rows], misc_recv.at[4])
    for i in range(D // 128):
        cols = pl.ds(i * 128, 128)
        nt[cols, sib_rows] = na[sib_rows, cols].T
    await_bytes(halo.at[oc], misc_recv.at[5])
    h0, h1 = iota((128, 128), 0), iota((128, 128), 1)
    source = ((h0 % 4) * 32) + ((h0 // 4) % 2) * 16 + h0 // 8
    halo_order = one_hot(source == h1)
    na[512:640, :] = dot(halo_order, halo[...].reshape(128, D)).astype(BF16)

    await_bytes(cot_sib, misc_recv.at[0])
    cp[c] = dot(to_phase, cot_vm[:, pl.ds(pl.multiple_of(c * H, H), H)]).astype(BF16)
    cp[oc] = dot(to_phase, cot_sib[...]).astype(BF16)
    c0, c1 = iota((128, 64), 0), iota((128, 64), 1)
    edge_order = one_hot(
        jnp.logical_and(c0 % 8 < 4, (c0 % 8) * 16 + c0 // 8 == c1)
    )
    await_bytes(cot_halo, misc_recv.at[1])
    cph[...] = dot(edge_order, cot_halo[...].reshape(64, H)).astype(BF16)

    ra = iota((ROWS, 128), 0)
    frame = frame0 + (ra % 8) * 32 + ra // 8
    hr = iota((128, 128), 0)
    place, q = hr % 8, hr // 8
    first_half = jnp.where(place % 2 == 0, q - 16, q + ROWS) + frame0
    halo_frame = jnp.where(place % 2 == 0, q - 32, q + ROWS) + (place // 4) * 16 + frame0

    def valid(flag):
        return jnp.where(flag, jnp.float32(1.0), jnp.float32(0.0))

    def masks(out, limits, edge):
        for u in (0, 1):
            out[u * ROWS : (u + 1) * ROWS, :] = valid(frame < limits[u : u + 1])
        limit = jnp.where((place // 2) % 2 == 0, limits[0:1], limits[1:2])
        out[512:640, :] = valid(jnp.logical_and(edge >= 0, edge < limit))

    masks(msk, fb_s[1, 2:4], halo_frame)

    from_phase = one_hot((r1i % 8) * 32 + r1i // 8 == r0)

    def stage1_start(j):
        for d in (1, 2, 3):
            send(g.at[j, 0, :, zd(d)], r1.at[j, 0, d - 1], r1_send.at[j, 0], r1_recv.at[j, 0],
                 dev(c, zd(d), y, x))
            send(g.at[j, 1, :, :, yd(d)], r1.at[j, 1, d - 1], r1_send.at[j, 1], r1_recv.at[j, 1],
                 dev(c, z, yd(d), x))

    def stage1_finish(j):
        for part in (0, 1):
            await_bytes(r1.at[j, part], r1_recv.at[j, part])

            def add(i, _):
                a, b = i // 4, i % 4
                mine = g[j, 0, a, z, b] if part == 0 else g[j, 1, a, b, y]
                total = mine.astype(F32)
                for d in range(3):
                    total = total + r1[j, part, d, a, b].astype(F32)
                s1[j, part, a, b] = total.astype(BF16)
                return 0

            lax.fori_loop(0, 8, add, 0)
        for d in (1, 2, 3):
            send(s1.at[j, 0, :, yd(d)], r2.at[j, 0, d - 1], r2_send.at[j, 0], r2_recv.at[j, 0],
                 dev(c, z, yd(d), x))
            send(s1.at[j, 1, :, zd(d)], r2.at[j, 1, d - 1], r2_send.at[j, 1], r2_recv.at[j, 1],
                 dev(c, zd(d), y, x))

    def stage2_finish(j):
        for part in (0, 1):
            await_bytes(r2.at[j, part], r2_recv.at[j, part])
            lanes = pl.ds(pl.multiple_of((j % 2) * 256 + part * 128, 128), 128)
            for a in (0, 1):
                total = s1[j, part, a, y if part == 0 else z].astype(F32)
                for d in range(3):
                    total = total + r2[j, part, d, a].astype(F32)
                sf[a, 0:48] = total
                for b in range(4):
                    fs[j // 2, a, b, :, lanes] = sf[a, 12 * b : 12 * b + 16].astype(BF16)

    def stage3_start(q, width):
        for e in (0, 1):
            core = c if e == 0 else oc
            for d in range(4):
                if e == 0 and d == 0:
                    continue
                send(fs.at[q, core, xd(d), :, pl.ds(0, width)], r3.at[q, e, d, :, pl.ds(0, width)],
                     r3_send.at[q, e], r3_recv.at[q, e], dev(core, z, y, xd(d)))

    def stage3_await(q, width, sems):
        await_bytes(r3.at[q, 0, 1:4, :, pl.ds(0, width)], sems.at[q, 0])
        await_bytes(r3.at[q, 1, :, :, pl.ds(0, width)], sems.at[q, 1])

    def stage3_finish(q, width):
        stage3_await(q, width, r3_recv)
        r3[q, 0, 0] = fs[q, c, x]
        squares = jnp.zeros((12, 128), F32)
        for e in (0, 1):
            core = c if e == 0 else oc
            for i in range(4):
                total = r3[q, e, 0, :, i * 128 : (i + 1) * 128].astype(F32)
                for d in range(1, 4):
                    total = total + r3[q, e, d, :, i * 128 : (i + 1) * 128].astype(F32)
                total = total[0:12]
                squares = squares + total * total
                at = pl.multiple_of((i % 2) * D + core * H + (2 * q + i // 2) * CH, CH)
                gin_vm[:, pl.ds(at, CH)] = total
        return squares

    sf[...] = jnp.zeros_like(sf)
    tg[...] = jnp.zeros_like(tg)
    for a in (0, 1):
        for b in range(4):
            fs[2, a, b, :, 512:640] = jnp.zeros((16, 128), BF16)

    sub = iota((16, 8, 128), 1)

    def chunk(j, _):
        lanes = pl.ds(pl.multiple_of(j * CH, CH), CH)
        for k in range(KT):
            tb[k] = jnp.broadcast_to(tapf[k : k + 1, lanes], (8, 128))
        await_w(j)
        pre[...] = dot(na[...], w_vm[j])

        def gated(rows):
            sig = sigmoid(pre[rows, CH:])
            val = pre[rows, :CH]
            return val, sig, val * sig * msk[rows, :]

        main = []
        for u in (0, 1):
            rows = slice(u * ROWS, (u + 1) * ROWS)
            val, sig, glued = gated(rows)
            val_s[rows, :] = val
            sig_s[rows, :] = sig
            xe[u, 16:48] = glued.reshape(32, 8, CH)
        h3 = gated(slice(512, 640))[2].reshape(16, 8, CH)
        h4 = pltpu.roll(h3, 4, 1)
        for u in (0, 1):
            left = h4 if u == 0 else pltpu.roll(h3, 2, 1)
            xe[u, 0:16] = jnp.where(sub == 0, left, pltpu.roll(xe[u, 32:48], 1, 1))
            xe[u, 48:64] = jnp.where(
                sub == 7, pltpu.roll(h3, 6 - 2 * u, 1), pltpu.roll(xe[u, 16:32], 7, 1)
            )
        xh[0:16] = jnp.where(
            sub == 1, pltpu.roll(xe[0, 32:48], 2, 1),
            jnp.where(sub == 3, pltpu.roll(xe[1, 32:48], 4, 1), h3),
        )
        xh[16:32] = jnp.where(sub % 2 == 0, h4, h3)
        xh[32:48] = jnp.where(
            sub == 0, xe[0, 16:32], jnp.where(sub == 2, pltpu.roll(xe[1, 16:32], 2, 1), h4)
        )

        def conv(window):
            total = tb[0][None] * window[0:8]
            for k in range(1, KT):
                total = total + tb[k][None] * window[k : k + 8]
            return total

        def through_swish(total, cot):
            gate = sigmoid(total)
            return cot * gate * (1.0 + total * (1.0 - gate))

        def forward(i, _):
            u, b = i // 4, i % 4
            total = conv(xe[u, pl.ds(b * 8, 39)])
            cot = cp[u, pl.ds(pl.multiple_of(b * 64, 64), 64), lanes].astype(F32)
            cot = cot * keep[pl.ds(pl.multiple_of(i * 64, 64), 64), :]
            de[u, pl.ds(16 + b * 8, 8)] = through_swish(total, cot.reshape(8, 8, CH))
            return 0

        @pl.when(j == 0)
        def _():
            await_bytes(fb_r.at[2], fb_recv.at[2])
            votes = jnp.minimum(
                jnp.minimum(fb_s[2], fb_r[2, 0]), jnp.minimum(fb_r[2, 1], fb_r[2, 2])
            )
            masks(keep, votes, first_half)

        lax.fori_loop(0, 8, forward, 0)

        def forward_edge(b, _):
            total = conv(xh[pl.ds(b * 8, 39)])
            cot = cph[pl.ds(pl.multiple_of(b * 64, 64), 64), lanes].astype(F32)
            cot = cot * keep[pl.ds(pl.multiple_of(512 + b * 64, 64), 64), :]
            dh[pl.ds(b * 8, 8)] = through_swish(total, cot.reshape(8, 8, CH))
            return 0

        lax.fori_loop(0, 2, forward_edge, 0)
        d3 = dh[...]
        for u in (0, 1):
            left = d3 if u == 0 else pltpu.roll(d3, 6, 1)
            de[u, 0:16] = jnp.where(sub == 0, left, pltpu.roll(de[u, 32:48], 1, 1))
            de[u, 48:64] = jnp.where(
                sub == 7, pltpu.roll(d3, 6 - 2 * u, 1), pltpu.roll(de[u, 16:32], 7, 1)
            )

        def backward(i, _):
            u, b = i // 4, i % 4
            window = de[u, pl.ds(b * 8 + 1, 39)]
            total = tb[0][None] * window[31:39]
            for k in range(1, KT):
                total = total + tb[k][None] * window[31 - k : 39 - k]
            rows = pl.ds(pl.multiple_of(i * 64, 64), 64)
            dglued = total.reshape(64, CH) * msk[rows, :]
            val, sig = val_s[rows, :], sig_s[rows, :]
            dval = dglued * sig
            dp[rows, 0:CH] = dval.astype(BF16)
            dp[rows, CH:] = (dval * val * (1.0 - sig)).astype(BF16)
            return 0

        lax.fori_loop(0, 8, backward, 0)

        def tap_terms(i, total):
            u, b = i // 4, i % 4
            window = xe[u, pl.ds(b * 8, 39)]
            grads = de[u, pl.ds(16 + b * 8, 8)]
            for m in range(8):
                total = total + grads[m][None] * window[m : m + 32]
            return total

        terms = lax.fori_loop(0, 8, tap_terms, jnp.zeros((KT, 8, CH), F32))
        tg[j, 0:KT] = jnp.sum(terms, axis=1)

        for i in range(8):
            grad = dot(nt[i * 192 : (i + 1) * 192, :], dp[...])
            for part in (0, 1):
                half = grad[:, part * CH : (part + 1) * CH].astype(BF16)
                g[j, part, i // 4, i % 4] = half.reshape(4, 48, CH)
        stage1_start(j)
        for u in (0, 1):
            rows = slice(u * ROWS, (u + 1) * ROWS)
            dpn[j, rows, :] = dot(from_phase, dp[rows, :]).astype(BF16)

        @pl.when(j >= 1)
        def _():
            stage1_finish(j - 1)

        @pl.when(j >= 2)
        def _():
            stage2_finish(j - 2)

        @pl.when(jnp.logical_and(j >= 3, j % 2 == 1))
        def _():
            stage3_start((j - 3) // 2, 512)

        return 0

    lax.fori_loop(0, NC, chunk, 0)

    for j in range(NC):
        tt[j * CH : (j + 1) * CH, :] = tg[j].T.astype(BF16)
    for d in (1, 2, 3):
        send(tt.at[pl.ds(pl.multiple_of(zd(d) * 192, 16), 192)], t_r1.at[d - 1],
             t_send.at[0], t_recv.at[0], dev(c, zd(d), y, x))

    dims = (((1,), (1,)), ((), ()))

    def dnormed(u, cols):
        rows = pl.ds(pl.multiple_of(u * ROWS, ROWS), ROWS)
        total = dot(dpn[0, rows, :], w_vm[0, cols, :], dims)
        for j in range(1, NC):
            total = total + dot(dpn[j, rows, :], w_vm[j, cols, :], dims)
        return total

    def sibling_part(i, _):
        cols = pl.ds(pl.multiple_of(i * 256, 256), 256)
        dns[:, cols] = dnormed(oc, cols).astype(BF16)
        return 0

    lax.fori_loop(0, D // 256, sibling_part, 0)
    send(dns, dnr, misc_send.at[6], misc_recv.at[6], sibling)

    stage1_finish(NC - 1)
    stage2_finish(NC - 2)
    await_bytes(t_r1, t_recv.at[0])
    mine = tt[pl.ds(pl.multiple_of(z * 192, 16), 192), :].astype(F32)
    for d in range(3):
        mine = mine + t_r1[d].astype(F32)
    t_s1[...] = mine.astype(BF16)
    for d in (1, 2, 3):
        send(t_s1.at[pl.ds(pl.multiple_of(yd(d) * 48, 16), 48)], t_r2.at[d - 1],
             t_send.at[1], t_recv.at[1], dev(c, z, yd(d), x))

    def own_part(i, _):
        cols = pl.ds(pl.multiple_of(i * 256, 256), 256)
        dno[:, cols] = dnormed(c, cols)
        return 0

    lax.fori_loop(0, D // 256, own_part, 0)

    stage2_finish(NC - 1)
    await_bytes(t_r2, t_recv.at[1])
    mine = t_s1[pl.ds(pl.multiple_of(y * 48, 16), 48), :].astype(F32)
    for d in range(3):
        mine = mine + t_r2[d].astype(F32)
    sf[0, 0:48] = mine
    for b in range(4):
        fs[2, c, b, :, 512:640] = sf[0, 12 * b : 12 * b + 16].astype(BF16)

    stage3_start(2, 640)

    await_bytes(dnr, misc_recv.at[6])

    def input_rows(i, _):
        rows = pl.ds(pl.multiple_of(i * 32, 32), 32)
        average, inverse = stat[0, rows, 0:1], stat[1, rows, 0:1]
        xhat = (x_vm[rows, :].astype(F32) - average) * inverse
        grad = dno[rows, :] + dnr[rows, :].astype(F32)
        m1 = jnp.mean(grad, axis=-1, keepdims=True)
        m2 = jnp.mean(grad * xhat, axis=-1, keepdims=True)
        gx_vm[rows, :] = (inverse * (grad - m1 - xhat * m2)).astype(BF16)
        return 0

    lax.fori_loop(0, ROWS // 32, input_rows, 0)
    store_gx = pltpu.make_async_copy(gx_vm, gx_hbm.at[0], local_sem.at[0])
    store_gx.start()

    squares = stage3_finish(0, 512) + stage3_finish(1, 512) + stage3_finish(2, 640)
    total = r3[2, 0, 0, :, 512:640].astype(F32)
    for d in range(1, 4):
        total = total + r3[2, 0, d, :, 512:640].astype(F32)
    tap_rows = total[0:12]
    squares = squares + tap_rows * tap_rows

    part = jnp.sum(jnp.sum(squares, axis=0, keepdims=True), axis=1, keepdims=True)
    ps_s[0] = jnp.broadcast_to(part, (8, 128))
    count = 0
    for e in (0, 1):
        for d in range(4):
            if e == 0 and d == 0:
                continue
            send(ps_s.at[0], ps_r.at[count], ps_send.at[0], ps_recv.at[0],
                 dev(c if e == 0 else oc, z, y, xd(d)))
            count += 1
    await_bytes(ps_r.at[0:7], ps_recv.at[0])
    total = ps_s[0]
    for i in range(7):
        total = total + ps_r[i]
    ps_s[1] = total
    for d in (1, 2, 3):
        send(ps_s.at[1], ps_r.at[6 + d], ps_send.at[1], ps_recv.at[1], dev(c, z, yd(d), x))
    await_bytes(ps_r.at[7:10], ps_recv.at[1])
    total = ps_s[1] + ps_r[7] + ps_r[8] + ps_r[9]
    ps_s[2] = total
    for d in (1, 2, 3):
        send(ps_s.at[2], ps_r.at[9 + d], ps_send.at[2], ps_recv.at[2], dev(c, zd(d), y, x))
    await_bytes(ps_r.at[10:13], ps_recv.at[2])
    total = ps_s[2] + ps_r[10] + ps_r[11] + ps_r[12]
    msq = total[0:1, 0:1] / jnp.float32(2 * D * D + D * KT)
    scale = 1.0 / jnp.maximum(jnp.float32(1.0), jnp.sqrt(msq))
    gin_vm[...] = gin_vm[...] * scale
    gtap_vm[...] = (tap_rows * scale)[:, 0:KT]
    store_gin = pltpu.make_async_copy(gin_vm, gin_hbm, local_sem.at[1])
    store_gin.start()
    store_gtap = pltpu.make_async_copy(gtap_vm, gtap_hbm, local_sem.at[2])
    store_gtap.start()

    for j in range(NC):
        await_bytes(w_vm.at[j, pl.ds(0, H)], w_send.at[j])
        for part in (0, 1):
            await_bytes(r1.at[j, part], r1_send.at[j, part])
            await_bytes(r2.at[j, part], r2_send.at[j, part])
    await_bytes(cot_sib, misc_send.at[0])
    await_bytes(cot_halo, misc_send.at[1])
    await_bytes(tap_in, misc_send.at[2])
    await_bytes(edges, misc_send.at[3])
    await_bytes(na.at[own_rows], misc_send.at[4])
    await_bytes(halo.at[c], misc_send.at[5])
    await_bytes(dns, misc_send.at[6])
    for i in range(3):
        await_bytes(fb_r.at[i], fb_send.at[i])
    for q, width in ((0, 512), (1, 512), (2, 640)):
        stage3_await(q, width, r3_send)
    await_bytes(t_r1, t_send.at[0])
    await_bytes(t_r2, t_send.at[1])
    await_bytes(ps_r.at[0:7], ps_send.at[0])
    await_bytes(ps_r.at[7:10], ps_send.at[1])
    await_bytes(ps_r.at[10:13], ps_send.at[2])
    store_gx.wait()
    store_gin.wait()
    store_gtap.wait()


def hand_over(gx, gin, gtap, gx_out, gin_out, gtap_out):
    gx_out[...] = gx[...]
    gin_out[...] = gin[...]
    gtap_out[...] = gtap[...]


def body(activations, cotangent, lengths, poison, w_in, taps):
    vmem = pltpu.VMEM
    dma = pltpu.SemaphoreType.DMA
    scratch = [
        vmem((ROWS, D), BF16),
        vmem((ROWS, D), BF16),
        vmem((ROWS, H), BF16),
        vmem((2, 2, 16, H), BF16),
        vmem((2, 32, D), BF16),
        vmem((ROWS, D), BF16),
        vmem((2, 2, 32, D), BF16),
        vmem((640, D), BF16),
        vmem((D, 512), BF16),
        vmem((NC, D, 2 * CH), BF16),
        vmem((2, ROWS, H), BF16),
        vmem((128, H), BF16),
        vmem((KT, H), BF16),
        vmem((KT, H), F32),
        vmem((KT, 8, CH), F32),
        vmem((640, 128), F32),
        vmem((640, 128), F32),
        vmem((2, ROWS, 128), F32),
        vmem((640, 2 * CH), F32),
        vmem((512, CH), F32),
        vmem((512, CH), F32),
        vmem((2, 64, 8, CH), F32),
        vmem((48, 8, CH), F32),
        vmem((2, 64, 8, CH), F32),
        vmem((16, 8, CH), F32),
        vmem((512, 2 * CH), BF16),
        vmem((NC, 512, 2 * CH), BF16),
        vmem((NC, 128, CH), F32),
        vmem((H, 128), BF16),
        vmem((NC, 2, 2, 4, 4, 48, CH), BF16),
        vmem((NC, 2, 3, 2, 4, 48, CH), BF16),
        vmem((NC, 2, 2, 4, 48, CH), BF16),
        vmem((NC, 2, 3, 2, 48, CH), BF16),
        vmem((3, 2, 4, 16, 640), BF16),
        vmem((3, 2, 4, 16, 640), BF16),
        vmem((2, 56, CH), F32),
        vmem((3, 192, 128), BF16),
        vmem((192, 128), BF16),
        vmem((3, 48, 128), BF16),
        vmem((ROWS, D), F32),
        vmem((ROWS, D), BF16),
        vmem((ROWS, D), BF16),
        vmem((ROWS, D), BF16),
        vmem((12, 2 * D), F32),
        vmem((12, KT), F32),
        vmem((3, 8, 128), jnp.int32),
        vmem((3, 3, 8, 128), jnp.int32),
        vmem((3, 8, 128), F32),
        vmem((13, 8, 128), F32),
        dma((3,)),
        dma((NC,)), dma((NC,)), dma((NC, 2)),
        dma((7,)), dma((7,)),
        dma((3,)), dma((3,)),
        dma((NC, 2)), dma((NC, 2)),
        dma((NC, 2)), dma((NC, 2)),
        dma((3, 2)), dma((3, 2)),
        dma((2,)), dma((2,)),
        dma((3,)), dma((3,)),
    ]
    anywhere = pl.BlockSpec(memory_space=pl.ANY)
    in_vmem = pl.BlockSpec(memory_space=pltpu.VMEM)
    in_smem = pl.BlockSpec(memory_space=pltpu.SMEM)
    shapes = (
        jax.ShapeDtypeStruct((1, ROWS, D), BF16),
        jax.ShapeDtypeStruct((12, 2 * D), F32),
        jax.ShapeDtypeStruct((12, KT), F32),
    )
    results = pl.pallas_call(
        kernel,
        out_shape=shapes,
        in_specs=[in_smem, in_smem, in_vmem, anywhere, anywhere, anywhere],
        out_specs=(anywhere, anywhere, anywhere),
        scratch_shapes=scratch,
        compiler_params=pltpu.CompilerParams(
            collective_id=0, has_side_effects=True, vmem_limit_bytes=56 * 1024 * 1024
        ),
        name="conformer_conv",
    )(lengths, poison, taps.T, activations, cotangent, w_in)
    return pl.pallas_call(
        hand_over,
        out_shape=shapes,
        in_specs=[in_vmem] * 3,
        out_specs=(in_vmem,) * 3,
        name="hand_over",
    )(*results)


def solution(mesh):
    placed = (
        P(("dp", "fsdp"), "seq", None),
        P(("dp", "fsdp"), "seq", None),
        P(("dp", "fsdp")),
        P(("dp", "fsdp"), "seq"),
        P("fsdp", None),
        P("fsdp", None),
    )
    return jax.shard_map(
        body,
        mesh=mesh,
        in_specs=placed,
        out_specs=(
            P(("dp", "fsdp"), "seq", None),
            P(("dp", "seq", "fsdp"), None),
            P(("dp", "seq", "fsdp"), None),
        ),
        check_vma=False,
    )
```

```python
import functools

import jax
import jax.numpy as jnp
from jax import lax
from jax.experimental import pallas as pl
from jax.experimental.pallas import tpu as pltpu
from jax.sharding import PartitionSpec as P

MESH = pl.DeviceIdType.MESH
F32 = jnp.float32
BF16 = jnp.bfloat16

D = 1536
H = 768
KT = 32
ROWS = 256
FRAMES = 8192
NC = 6
CH = 128
BIG = FRAMES


def sigmoid(v):
    return 0.5 * jnp.tanh(0.5 * v) + 0.5


def dot(a, b, dims=(((1,), (0,)), ((), ()))):
    return lax.dot_general(a, b, dims, preferred_element_type=F32)


def iota(shape, dim):
    return lax.broadcasted_iota(jnp.int32, shape, dim)


def one_hot(flag):
    return jnp.where(flag, jnp.float32(1.0), jnp.float32(0.0)).astype(BF16)


def await_bytes(ref, sem):
    pltpu.make_async_copy(ref, ref, sem).wait()


def kernel(
    len_ref, poi_ref, taps_ref, x_hbm, cot_hbm, w_hbm,
    gx_hbm, gin_hbm, gtap_hbm,
    x_vm, cot_vm, cot_sib, cot_halo, edges, nn, halo, na, nt, w_vm, cp, cph,
    tap_in, tapf, tb, msk, keep, stat, pre, val_s, sig_s, xe, xh, de, dh, dp, dpn,
    tg, tt, g, rd, s1, r2, fs, r3, sf, t_r1, t_s1, t_r2,
    dno, dns, dnr, gx_vm, gin_vm, gtap_vm, fb_s, fb_r, ps_s, ps_r,
    local_sem, w_loc, w_send, w_recv, misc_send, misc_recv, fb_send, fb_recv,
    rd_send, rd_recv, r2_send, r2_recv, r3_send, r3_recv, t_send, t_recv, ps_send, ps_recv,
):
    c = lax.axis_index("dp")
    s = lax.axis_index("seq")
    f = lax.axis_index("fsdp")
    z, y = s // 8, (s // 2) % 4
    x = (s % 2) * 2 + f
    oc = 1 - c

    def dev(core, zz, yy, xx):
        return (core, zz * 8 + yy * 2 + xx // 2, xx % 2)

    def xd(d):
        return (x + d) % 4

    def yd(d):
        return (y + d) % 4

    def zd(d):
        return (z + d) % 4

    nxt, prv = (s + 1) % 32, (s + 31) % 32
    sibling = dev(oc, z, y, x)

    def send(src, dst, send_sem, recv_sem, device):
        pltpu.make_async_remote_copy(
            src_ref=src, dst_ref=dst, send_sem=send_sem, recv_sem=recv_sem,
            device_id=device, device_id_type=MESH,
        ).start()

    partners = [sibling]
    partners += [dev(e, z, y, xd(d)) for d in (1, 2, 3) for e in (0, 1)]
    partners += [dev(c, z, yd(d), x) for d in (1, 2, 3)]
    partners += [dev(c, zd(d), y, x) for d in (1, 2, 3)]
    partners += [(e, q, f) for q in (prv, nxt) for e in (0, 1)]
    barrier = pltpu.get_barrier_semaphore()
    for partner in partners:
        pl.semaphore_signal(barrier, inc=1, device_id=partner, device_id_type=MESH)

    load_x = pltpu.make_async_copy(x_hbm.at[0], x_vm, local_sem.at[0])
    load_cot = pltpu.make_async_copy(cot_hbm.at[0], cot_vm, local_sem.at[1])
    load_cot.start()
    load_x.start()

    def w_columns(j, part):
        return pl.ds(pl.multiple_of(part * D + c * H + j * CH, CH), CH)

    def local_w(j):
        for part in (0, 1):
            pltpu.make_async_copy(
                w_hbm.at[:, w_columns(j, part)],
                w_vm.at[j, pl.ds(pl.multiple_of(f * H, H), H), pl.ds(part * CH, CH)],
                w_loc.at[j],
            ).start()

    def send_w(j):
        for side in (0, 1):
            for part in (0, 1):
                send(
                    w_hbm.at[pl.ds(side * (H // 2), H // 2), w_columns(j, part)],
                    w_vm.at[
                        j,
                        pl.ds(pl.multiple_of(f * H + side * (H // 2), H // 2), H // 2),
                        pl.ds(part * CH, CH),
                    ],
                    w_send.at[j], w_recv.at[j, side], dev(c, z, y, xd(1 if side == 0 else 3)),
                )

    def await_w(j):
        await_bytes(w_vm.at[j, pl.ds(pl.multiple_of(f * H, H), H)], w_loc.at[j])
        for side in (0, 1):
            base = pl.multiple_of((1 - f) * H + side * (H // 2), H // 2)
            await_bytes(w_vm.at[j, pl.ds(base, H // 2)], w_recv.at[j, side])

    for j in range(NC):
        local_w(j)

    frame0 = s * ROWS
    load_cot.wait()
    spoiled = jnp.zeros((ROWS, 128), F32)
    for i in range(D // 128):
        spoiled = spoiled + cot_vm[:, i * 128 : (i + 1) * 128].astype(F32) * 0.0
    local = iota((ROWS, 128), 0)
    bad = jnp.logical_or(spoiled != 0.0, local == poi_ref[0, 0])
    cand = jnp.where(bad, frame0 + local, jnp.int32(BIG))
    cand = jnp.min(cand.reshape(ROWS // 8, 8, 128), axis=0)
    cand = jnp.min(jnp.min(cand, axis=0, keepdims=True), axis=1, keepdims=True)
    row = iota((8, 128), 0)
    tile = jnp.where(row == c, jnp.broadcast_to(cand, (8, 128)), jnp.int32(BIG))
    fb_s[0] = jnp.where(row == 2 + c, len_ref[0], tile)

    pl.semaphore_wait(barrier, len(partners))

    for k, partner in enumerate((sibling, dev(c, z, y, xd(2)), dev(oc, z, y, xd(2)))):
        send(fb_s.at[0], fb_r.at[0, k], fb_send.at[0], fb_recv.at[0], partner)
    send(x_hbm.at[0, pl.ds(ROWS - 32, 32)], edges.at[0], misc_send.at[3], misc_recv.at[3], (c, nxt, f))
    send(x_hbm.at[0, pl.ds(0, 32)], edges.at[1], misc_send.at[3], misc_recv.at[3], (c, prv, f))
    send(
        cot_vm.at[:, pl.ds(pl.multiple_of(oc * H, H), H)], cot_sib,
        misc_send.at[0], misc_recv.at[0], sibling,
    )
    for e in (0, 1):
        cols = pl.ds(e * H, H)
        send(cot_vm.at[pl.ds(ROWS - 16, 16), cols], cot_halo.at[c, 0],
             misc_send.at[1], misc_recv.at[1], (e, nxt, f))
        send(cot_vm.at[pl.ds(0, 16), cols], cot_halo.at[c, 1],
             misc_send.at[1], misc_recv.at[1], (e, prv, f))
    send(taps_ref, tap_in, misc_send.at[2], misc_recv.at[2], dev(c, z, y, xd(3)))
    for j in range(NC):
        send_w(j)

    load_x.wait()

    def normalised(frames):
        xf = frames.astype(F32)
        average = jnp.mean(xf, axis=-1, keepdims=True)
        cent = xf - average
        inverse = lax.rsqrt(jnp.mean(cent * cent, axis=-1, keepdims=True) + 1e-05)
        return (cent * inverse).astype(BF16), average, inverse

    def norm_rows(i, _):
        rows = pl.ds(pl.multiple_of(i * 32, 32), 32)
        nn[rows, :], average, inverse = normalised(x_vm[rows, :])
        stat[0, rows, :] = jnp.broadcast_to(average, (32, 128))
        stat[1, rows, :] = jnp.broadcast_to(inverse, (32, 128))
        return 0

    lax.fori_loop(0, ROWS // 32, norm_rows, 0)

    r0, r1i = iota((ROWS, ROWS), 0), iota((ROWS, ROWS), 1)
    to_phase = one_hot((r0 % 8) * 32 + r0 // 8 == r1i)
    own_rows = pl.ds(pl.multiple_of(c * ROWS, ROWS), ROWS)
    sib_rows = pl.ds(pl.multiple_of(oc * ROWS, ROWS), ROWS)
    na[own_rows, :] = dot(to_phase, nn[...]).astype(BF16)
    send(na.at[own_rows], na.at[own_rows], misc_send.at[4], misc_recv.at[4], sibling)

    await_bytes(fb_r.at[0], fb_recv.at[0])
    fb_s[1] = jnp.minimum(jnp.minimum(fb_s[0], fb_r[0, 0]), jnp.minimum(fb_r[0, 1], fb_r[0, 2]))
    for d in (1, 2, 3):
        send(fb_s.at[1], fb_r.at[1, d - 1], fb_send.at[1], fb_recv.at[1], dev(c, z, yd(d), x))

    for i in range(D // 128):
        cols = pl.ds(i * 128, 128)
        nt[cols, own_rows] = na[own_rows, cols].T

    await_bytes(edges, misc_recv.at[3])
    for side in (0, 1):
        halo[c, side] = normalised(edges[side])[0]
    send(halo.at[c], halo.at[c], misc_send.at[5], misc_recv.at[5], sibling)

    await_bytes(fb_r.at[1], fb_recv.at[1])
    fb_s[2] = jnp.minimum(jnp.minimum(fb_s[1], fb_r[1, 0]), jnp.minimum(fb_r[1, 1], fb_r[1, 2]))
    for d in (1, 2, 3):
        send(fb_s.at[2], fb_r.at[2, d - 1], fb_send.at[2], fb_recv.at[2], dev(c, zd(d), y, x))

    await_bytes(tap_in, misc_recv.at[2])
    mine = jnp.where(f == c, jnp.float32(1.0), jnp.float32(0.0))
    tapf[...] = taps_ref[...].astype(F32) * mine + tap_in[...].astype(F32) * (1.0 - mine)

    await_bytes(na.at[sib_rows], misc_recv.at[4])
    for i in range(D // 128):
        cols = pl.ds(i * 128, 128)
        nt[cols, sib_rows] = na[sib_rows, cols].T
    await_bytes(halo.at[oc], misc_recv.at[5])
    h0, h1 = iota((128, 128), 0), iota((128, 128), 1)
    source = ((h0 % 4) * 32) + ((h0 // 4) % 2) * 16 + h0 // 8
    halo_order = one_hot(source == h1)
    na[512:640, :] = dot(halo_order, halo[...].reshape(128, D)).astype(BF16)

    await_bytes(cot_sib, misc_recv.at[0])
    cp[c] = dot(to_phase, cot_vm[:, pl.ds(pl.multiple_of(c * H, H), H)]).astype(BF16)
    cp[oc] = dot(to_phase, cot_sib[...]).astype(BF16)
    c0, c1 = iota((128, 64), 0), iota((128, 64), 1)
    edge_order = one_hot(
        jnp.logical_and(c0 % 8 < 4, (c0 % 8) * 16 + c0 // 8 == c1)
    )
    await_bytes(cot_halo, misc_recv.at[1])
    cph[...] = dot(edge_order, cot_halo[...].reshape(64, H)).astype(BF16)

    ri = iota((ROWS, 128), 0)
    frame = frame0 + (ri % 8) * 32 + ri // 8
    hr = iota((128, 128), 0)
    place, q = hr % 8, hr // 8
    first_half = jnp.where(place % 2 == 0, q - 16, q + ROWS) + frame0
    halo_frame = jnp.where(place % 2 == 0, q - 32, q + ROWS) + (place // 4) * 16 + frame0

    def valid(flag):
        return jnp.where(flag, jnp.float32(1.0), jnp.float32(0.0))

    def masks(out, limits, edge):
        for u in (0, 1):
            out[u * ROWS : (u + 1) * ROWS, :] = valid(frame < limits[u : u + 1])
        limit = jnp.where((place // 2) % 2 == 0, limits[0:1], limits[1:2])
        out[512:640, :] = valid(jnp.logical_and(edge >= 0, edge < limit))

    masks(msk, fb_s[1, 2:4], halo_frame)

    from_phase = one_hot((r1i % 8) * 32 + r1i // 8 == r0)

    def ring_dev(part, d):
        return dev(c, zd(d), y, x) if part == 0 else dev(c, z, yd(d), x)

    def direct_start(j):
        for part in (0, 1):
            for d in (1, 2, 3):
                src = g.at[j, 0, :, zd(d)] if part == 0 else g.at[j, 1, :, :, yd(d)]
                send(src, rd.at[j, part, d - 1], rd_send.at[j, part], rd_recv.at[j, part], ring_dev(part, d))

    def direct_finish(j):
        for part in (0, 1):
            await_bytes(rd.at[j, part], rd_recv.at[j, part])

            def add(i, _):
                a, b = i // 4, i % 4
                own = g[j, 0, a, z, b] if part == 0 else g[j, 1, a, b, y]
                total = own.astype(F32)
                for d in range(3):
                    total = total + rd[j, part, d, a, b].astype(F32)
                s1[j, part, a, b] = total.astype(BF16)
                return 0

            lax.fori_loop(0, 8, add, 0)
        stage2_start(j)

    def stage2_start(j):
        for d in (1, 2, 3):
            send(s1.at[j, 0, :, yd(d)], r2.at[j, 0, d - 1], r2_send.at[j, 0], r2_recv.at[j, 0],
                 dev(c, z, yd(d), x))
            send(s1.at[j, 1, :, zd(d)], r2.at[j, 1, d - 1], r2_send.at[j, 1], r2_recv.at[j, 1],
                 dev(c, zd(d), y, x))

    def stage2_finish(j):
        for part in (0, 1):
            await_bytes(r2.at[j, part], r2_recv.at[j, part])
            lanes = pl.ds(pl.multiple_of((j % 2) * 256 + part * 128, 128), 128)
            for a in (0, 1):
                total = s1[j, part, a, y if part == 0 else z].astype(F32)
                for d in range(3):
                    total = total + r2[j, part, d, a].astype(F32)
                sf[a, 0:48] = total
                for b in range(4):
                    fs[j // 2, a, b, :, lanes] = sf[a, 12 * b : 12 * b + 16].astype(BF16)

    def stage3_start(q, width):
        for e in (0, 1):
            core = c if e == 0 else oc
            for d in range(4):
                if e == 0 and d == 0:
                    continue
                send(fs.at[q, core, xd(d), :, pl.ds(0, width)], r3.at[q, e, d, :, pl.ds(0, width)],
                     r3_send.at[q, e], r3_recv.at[q, e], dev(core, z, y, xd(d)))

    def stage3_await(q, width, sems):
        await_bytes(r3.at[q, 0, 1:4, :, pl.ds(0, width)], sems.at[q, 0])
        await_bytes(r3.at[q, 1, :, :, pl.ds(0, width)], sems.at[q, 1])

    def stage3_finish(q, width):
        stage3_await(q, width, r3_recv)
        r3[q, 0, 0] = fs[q, c, x]
        squares = jnp.zeros((12, 128), F32)
        for e in (0, 1):
            core = c if e == 0 else oc
            for i in range(4):
                total = r3[q, e, 0, :, i * 128 : (i + 1) * 128].astype(F32)
                for d in range(1, 4):
                    total = total + r3[q, e, d, :, i * 128 : (i + 1) * 128].astype(F32)
                total = total[0:12]
                squares = squares + total * total
                at = pl.multiple_of((i % 2) * D + core * H + (2 * q + i // 2) * CH, CH)
                gin_vm[:, pl.ds(at, CH)] = total
        return squares

    sf[...] = jnp.zeros_like(sf)
    tg[...] = jnp.zeros_like(tg)
    for a in (0, 1):
        for b in range(4):
            fs[2, a, b, :, 512:640] = jnp.zeros((16, 128), BF16)

    sub = iota((16, 8, 128), 1)

    def chunk(j, _):
        lanes = pl.ds(pl.multiple_of(j * CH, CH), CH)
        for k in range(KT):
            tb[k] = jnp.broadcast_to(tapf[k : k + 1, lanes], (8, 128))
        await_w(j)
        pre[...] = dot(na[...], w_vm[j])

        def gated(rows):
            sig = sigmoid(pre[rows, CH:])
            val = pre[rows, :CH]
            return val, sig, val * sig * msk[rows, :]

        main = []
        for u in (0, 1):
            rows = slice(u * ROWS, (u + 1) * ROWS)
            val, sig, glued = gated(rows)
            val_s[rows, :] = val
            sig_s[rows, :] = sig
            xe[u, 16:48] = glued.reshape(32, 8, CH)
        h3 = gated(slice(512, 640))[2].reshape(16, 8, CH)
        h4 = pltpu.roll(h3, 4, 1)
        for u in (0, 1):
            left = h4 if u == 0 else pltpu.roll(h3, 2, 1)
            xe[u, 0:16] = jnp.where(sub == 0, left, pltpu.roll(xe[u, 32:48], 1, 1))
            xe[u, 48:64] = jnp.where(
                sub == 7, pltpu.roll(h3, 6 - 2 * u, 1), pltpu.roll(xe[u, 16:32], 7, 1)
            )
        xh[0:16] = jnp.where(
            sub == 1, pltpu.roll(xe[0, 32:48], 2, 1),
            jnp.where(sub == 3, pltpu.roll(xe[1, 32:48], 4, 1), h3),
        )
        xh[16:32] = jnp.where(sub % 2 == 0, h4, h3)
        xh[32:48] = jnp.where(
            sub == 0, xe[0, 16:32], jnp.where(sub == 2, pltpu.roll(xe[1, 16:32], 2, 1), h4)
        )

        def conv(window):
            total = tb[0][None] * window[0:8]
            for k in range(1, KT):
                total = total + tb[k][None] * window[k : k + 8]
            return total

        def through_swish(total, cot):
            gate = sigmoid(total)
            return cot * gate * (1.0 + total * (1.0 - gate))

        def forward(i, _):
            u, b = i // 4, i % 4
            total = conv(xe[u, pl.ds(b * 8, 39)])
            cot = cp[u, pl.ds(pl.multiple_of(b * 64, 64), 64), lanes].astype(F32)
            cot = cot * keep[pl.ds(pl.multiple_of(i * 64, 64), 64), :]
            de[u, pl.ds(16 + b * 8, 8)] = through_swish(total, cot.reshape(8, 8, CH))
            return 0

        @pl.when(j == 0)
        def _():
            await_bytes(fb_r.at[2], fb_recv.at[2])
            votes = jnp.minimum(
                jnp.minimum(fb_s[2], fb_r[2, 0]), jnp.minimum(fb_r[2, 1], fb_r[2, 2])
            )
            masks(keep, votes, first_half)

        lax.fori_loop(0, 8, forward, 0, unroll=4)

        def forward_edge(b, _):
            total = conv(xh[pl.ds(b * 8, 39)])
            cot = cph[pl.ds(pl.multiple_of(b * 64, 64), 64), lanes].astype(F32)
            cot = cot * keep[pl.ds(pl.multiple_of(512 + b * 64, 64), 64), :]
            dh[pl.ds(b * 8, 8)] = through_swish(total, cot.reshape(8, 8, CH))
            return 0

        lax.fori_loop(0, 2, forward_edge, 0)
        d3 = dh[...]
        for u in (0, 1):
            left = d3 if u == 0 else pltpu.roll(d3, 6, 1)
            de[u, 0:16] = jnp.where(sub == 0, left, pltpu.roll(de[u, 32:48], 1, 1))
            de[u, 48:64] = jnp.where(
                sub == 7, pltpu.roll(d3, 6 - 2 * u, 1), pltpu.roll(de[u, 16:32], 7, 1)
            )

        def backward(i, _):
            u, b = i // 4, i % 4
            window = de[u, pl.ds(b * 8 + 1, 39)]
            total = tb[0][None] * window[31:39]
            for k in range(1, KT):
                total = total + tb[k][None] * window[31 - k : 39 - k]
            rows = pl.ds(pl.multiple_of(i * 64, 64), 64)
            dglued = total.reshape(64, CH) * msk[rows, :]
            val, sig = val_s[rows, :], sig_s[rows, :]
            dval = dglued * sig
            dp[rows, 0:CH] = dval.astype(BF16)
            dp[rows, CH:] = (dval * val * (1.0 - sig)).astype(BF16)
            return 0

        lax.fori_loop(0, 8, backward, 0, unroll=4)

        for i in range(8):
            grad = dot(nt[i * 192 : (i + 1) * 192, :], dp[...])
            for part in (0, 1):
                half = grad[:, part * CH : (part + 1) * CH].astype(BF16)
                g[j, part, i // 4, i % 4] = half.reshape(4, 48, CH)

        direct_start(j)

        for h in (0, 16):

            def tap_terms(i, total):
                u, b = i // 4, i % 4
                window = xe[u, pl.ds(b * 8 + h, 23)]
                grads = de[u, pl.ds(16 + b * 8, 8)]
                for m in range(8):
                    total = total + grads[m][None] * window[m : m + 16]
                return total

            terms = lax.fori_loop(0, 8, tap_terms, jnp.zeros((16, 8, CH), F32), unroll=4)
            tg[j, h : h + 16] = jnp.sum(terms, axis=1)
        for u in (0, 1):
            rows = slice(u * ROWS, (u + 1) * ROWS)
            dpn[j, rows, :] = dot(from_phase, dp[rows, :]).astype(BF16)

        @pl.when(j >= 1)
        def _():
            direct_finish(j - 1)

        @pl.when(j >= 2)
        def _():
            stage2_finish(j - 2)

        @pl.when(jnp.logical_and(j >= 3, j % 2 == 1))
        def _():
            stage3_start((j - 3) // 2, 512)

        return 0

    lax.fori_loop(0, NC, chunk, 0)

    for j in range(NC):
        tt[j * CH : (j + 1) * CH, :] = tg[j].T.astype(BF16)
    for d in (1, 2, 3):
        send(tt.at[pl.ds(pl.multiple_of(zd(d) * 192, 16), 192)], t_r1.at[d - 1],
             t_send.at[0], t_recv.at[0], dev(c, zd(d), y, x))

    dims = (((1,), (1,)), ((), ()))

    def dnormed(u, cols):
        rows = pl.ds(pl.multiple_of(u * ROWS, ROWS), ROWS)
        total = dot(dpn[0, rows, :], w_vm[0, cols, :], dims)
        for j in range(1, NC):
            total = total + dot(dpn[j, rows, :], w_vm[j, cols, :], dims)
        return total

    def sibling_part(i, _):
        cols = pl.ds(pl.multiple_of(i * 256, 256), 256)
        dns[:, cols] = dnormed(oc, cols).astype(BF16)
        return 0

    lax.fori_loop(0, D // 256, sibling_part, 0)
    send(dns, dnr, misc_send.at[6], misc_recv.at[6], sibling)

    direct_finish(NC - 1)
    stage2_finish(NC - 2)
    await_bytes(t_r1, t_recv.at[0])
    mine = tt[pl.ds(pl.multiple_of(z * 192, 16), 192), :].astype(F32)
    for d in range(3):
        mine = mine + t_r1[d].astype(F32)
    t_s1[...] = mine.astype(BF16)
    for d in (1, 2, 3):
        send(t_s1.at[pl.ds(pl.multiple_of(yd(d) * 48, 16), 48)], t_r2.at[d - 1],
             t_send.at[1], t_recv.at[1], dev(c, z, yd(d), x))

    def own_part(i, _):
        cols = pl.ds(pl.multiple_of(i * 256, 256), 256)
        dno[:, cols] = dnormed(c, cols)
        return 0

    lax.fori_loop(0, D // 256, own_part, 0)

    stage2_finish(NC - 1)
    await_bytes(t_r2, t_recv.at[1])
    mine = t_s1[pl.ds(pl.multiple_of(y * 48, 16), 48), :].astype(F32)
    for d in range(3):
        mine = mine + t_r2[d].astype(F32)
    sf[0, 0:48] = mine
    for b in range(4):
        fs[2, c, b, :, 512:640] = sf[0, 12 * b : 12 * b + 16].astype(BF16)

    stage3_start(2, 640)

    await_bytes(dnr, misc_recv.at[6])

    def input_rows(i, _):
        rows = pl.ds(pl.multiple_of(i * 32, 32), 32)
        average, inverse = stat[0, rows, 0:1], stat[1, rows, 0:1]
        xhat = (x_vm[rows, :].astype(F32) - average) * inverse
        grad = dno[rows, :] + dnr[rows, :].astype(F32)
        m1 = jnp.mean(grad, axis=-1, keepdims=True)
        m2 = jnp.mean(grad * xhat, axis=-1, keepdims=True)
        gx_vm[rows, :] = (inverse * (grad - m1 - xhat * m2)).astype(BF16)
        return 0

    lax.fori_loop(0, ROWS // 32, input_rows, 0)
    store_gx = pltpu.make_async_copy(gx_vm, gx_hbm.at[0], local_sem.at[0])
    store_gx.start()

    squares = stage3_finish(0, 512) + stage3_finish(1, 512) + stage3_finish(2, 640)
    total = r3[2, 0, 0, :, 512:640].astype(F32)
    for d in range(1, 4):
        total = total + r3[2, 0, d, :, 512:640].astype(F32)
    tap_rows = total[0:12]
    squares = squares + tap_rows * tap_rows

    part = jnp.sum(jnp.sum(squares, axis=0, keepdims=True), axis=1, keepdims=True)
    ps_s[0] = jnp.broadcast_to(part, (8, 128))
    count = 0
    for e in (0, 1):
        for d in range(4):
            if e == 0 and d == 0:
                continue
            send(ps_s.at[0], ps_r.at[count], ps_send.at[0], ps_recv.at[0],
                 dev(c if e == 0 else oc, z, y, xd(d)))
            count += 1
    await_bytes(ps_r.at[0:7], ps_recv.at[0])
    total = ps_s[0]
    for i in range(7):
        total = total + ps_r[i]
    ps_s[1] = total
    for d in (1, 2, 3):
        send(ps_s.at[1], ps_r.at[6 + d], ps_send.at[1], ps_recv.at[1], dev(c, z, yd(d), x))
    await_bytes(ps_r.at[7:10], ps_recv.at[1])
    total = ps_s[1] + ps_r[7] + ps_r[8] + ps_r[9]
    ps_s[2] = total
    for d in (1, 2, 3):
        send(ps_s.at[2], ps_r.at[9 + d], ps_send.at[2], ps_recv.at[2], dev(c, zd(d), y, x))
    await_bytes(ps_r.at[10:13], ps_recv.at[2])
    total = ps_s[2] + ps_r[10] + ps_r[11] + ps_r[12]
    msq = total[0:1, 0:1] / jnp.float32(2 * D * D + D * KT)
    scale = 1.0 / jnp.maximum(jnp.float32(1.0), jnp.sqrt(msq))
    gin_vm[...] = gin_vm[...] * scale
    gtap_vm[...] = (tap_rows * scale)[:, 0:KT]
    store_gin = pltpu.make_async_copy(gin_vm, gin_hbm, local_sem.at[1])
    store_gin.start()
    store_gtap = pltpu.make_async_copy(gtap_vm, gtap_hbm, local_sem.at[2])
    store_gtap.start()

    for j in range(NC):
        await_bytes(w_vm.at[j, pl.ds(0, H)], w_send.at[j])
        for part in (0, 1):
            await_bytes(r2.at[j, part], r2_send.at[j, part])
    for j in range(NC):
        for part in (0, 1):
            await_bytes(rd.at[j, part], rd_send.at[j, part])
    await_bytes(cot_sib, misc_send.at[0])
    await_bytes(cot_halo, misc_send.at[1])
    await_bytes(tap_in, misc_send.at[2])
    await_bytes(edges, misc_send.at[3])
    await_bytes(na.at[own_rows], misc_send.at[4])
    await_bytes(halo.at[c], misc_send.at[5])
    await_bytes(dns, misc_send.at[6])
    for i in range(3):
        await_bytes(fb_r.at[i], fb_send.at[i])
    for q, width in ((0, 512), (1, 512), (2, 640)):
        stage3_await(q, width, r3_send)
    await_bytes(t_r1, t_send.at[0])
    await_bytes(t_r2, t_send.at[1])
    await_bytes(ps_r.at[0:7], ps_send.at[0])
    await_bytes(ps_r.at[7:10], ps_send.at[1])
    await_bytes(ps_r.at[10:13], ps_send.at[2])
    store_gx.wait()
    store_gin.wait()
    store_gtap.wait()


def hand_over(gx, gin, gtap, gx_out, gin_out, gtap_out):
    gx_out[...] = gx[...]
    gin_out[...] = gin[...]
    gtap_out[...] = gtap[...]


def body(activations, cotangent, lengths, poison, w_in, taps):
    vmem = pltpu.VMEM
    dma = pltpu.SemaphoreType.DMA
    scratch = [
        vmem((ROWS, D), BF16),
        vmem((ROWS, D), BF16),
        vmem((ROWS, H), BF16),
        vmem((2, 2, 16, H), BF16),
        vmem((2, 32, D), BF16),
        vmem((ROWS, D), BF16),
        vmem((2, 2, 32, D), BF16),
        vmem((640, D), BF16),
        vmem((D, 512), BF16),
        vmem((NC, D, 2 * CH), BF16),
        vmem((2, ROWS, H), BF16),
        vmem((128, H), BF16),
        vmem((KT, H), BF16),
        vmem((KT, H), F32),
        vmem((KT, 8, CH), F32),
        vmem((640, 128), F32),
        vmem((640, 128), F32),
        vmem((2, ROWS, 128), F32),
        vmem((640, 2 * CH), F32),
        vmem((512, CH), F32),
        vmem((512, CH), F32),
        vmem((2, 64, 8, CH), F32),
        vmem((48, 8, CH), F32),
        vmem((2, 64, 8, CH), F32),
        vmem((16, 8, CH), F32),
        vmem((512, 2 * CH), BF16),
        vmem((NC, 512, 2 * CH), BF16),
        vmem((NC, 128, CH), F32),
        vmem((H, 128), BF16),
        vmem((NC, 2, 2, 4, 4, 48, CH), BF16),
        vmem((NC, 2, 3, 2, 4, 48, CH), BF16),
        vmem((NC, 2, 2, 4, 48, CH), BF16),
        vmem((NC, 2, 3, 2, 48, CH), BF16),
        vmem((3, 2, 4, 16, 640), BF16),
        vmem((3, 2, 4, 16, 640), BF16),
        vmem((2, 56, CH), F32),
        vmem((3, 192, 128), BF16),
        vmem((192, 128), BF16),
        vmem((3, 48, 128), BF16),
        vmem((ROWS, D), F32),
        vmem((ROWS, D), BF16),
        vmem((ROWS, D), BF16),
        vmem((ROWS, D), BF16),
        vmem((12, 2 * D), F32),
        vmem((12, KT), F32),
        vmem((3, 8, 128), jnp.int32),
        vmem((3, 3, 8, 128), jnp.int32),
        vmem((3, 8, 128), F32),
        vmem((13, 8, 128), F32),
        dma((3,)),
        dma((NC,)), dma((NC,)), dma((NC, 2)),
        dma((7,)), dma((7,)),
        dma((3,)), dma((3,)),
        dma((NC, 2)), dma((NC, 2)),
        dma((NC, 2)), dma((NC, 2)),
        dma((3, 2)), dma((3, 2)),
        dma((2,)), dma((2,)),
        dma((3,)), dma((3,)),
    ]
    anywhere = pl.BlockSpec(memory_space=pl.ANY)
    in_vmem = pl.BlockSpec(memory_space=pltpu.VMEM)
    in_smem = pl.BlockSpec(memory_space=pltpu.SMEM)
    shapes = (
        jax.ShapeDtypeStruct((1, ROWS, D), BF16),
        jax.ShapeDtypeStruct((12, 2 * D), F32),
        jax.ShapeDtypeStruct((12, KT), F32),
    )
    results = pl.pallas_call(
        kernel,
        out_shape=shapes,
        in_specs=[in_smem, in_smem, in_vmem, anywhere, anywhere, anywhere],
        out_specs=(anywhere, anywhere, anywhere),
        scratch_shapes=scratch,
        compiler_params=pltpu.CompilerParams(
            collective_id=0, has_side_effects=True, vmem_limit_bytes=56 * 1024 * 1024
        ),
        name="conformer_conv",
    )(lengths, poison, taps.T, activations, cotangent, w_in)
    return pl.pallas_call(
        hand_over,
        out_shape=shapes,
        in_specs=[in_vmem] * 3,
        out_specs=(in_vmem,) * 3,
        name="hand_over",
    )(*results)


def solution(mesh):
    placed = (
        P(("dp", "fsdp"), "seq", None),
        P(("dp", "fsdp"), "seq", None),
        P(("dp", "fsdp")),
        P(("dp", "fsdp"), "seq"),
        P("fsdp", None),
        P("fsdp", None),
    )
    return jax.shard_map(
        body,
        mesh=mesh,
        in_specs=placed,
        out_specs=(
            P(("dp", "fsdp"), "seq", None),
            P(("dp", "seq", "fsdp"), None),
            P(("dp", "seq", "fsdp"), None),
        ),
        check_vma=False,
    )
```

```python
import functools

import jax
import jax.numpy as jnp
from jax import lax
from jax.experimental import pallas as pl
from jax.experimental.pallas import tpu as pltpu
from jax.sharding import PartitionSpec as P

MESH = pl.DeviceIdType.MESH
F32 = jnp.float32
BF16 = jnp.bfloat16

D = 1536
H = 768
KT = 32
ROWS = 256
FRAMES = 8192
NC = 6
CH = 128
BIG = FRAMES


def sigmoid(v):
    return 0.5 * jnp.tanh(0.5 * v) + 0.5


def dot(a, b, dims=(((1,), (0,)), ((), ()))):
    return lax.dot_general(a, b, dims, preferred_element_type=F32)


def iota(shape, dim):
    return lax.broadcasted_iota(jnp.int32, shape, dim)


def one_hot(flag):
    return jnp.where(flag, jnp.float32(1.0), jnp.float32(0.0)).astype(BF16)


def await_bytes(ref, sem):
    pltpu.make_async_copy(ref, ref, sem).wait()


def kernel(
    len_ref, poi_ref, taps_ref, x_hbm, cot_hbm, w_hbm,
    gx_hbm, gin_hbm, gtap_hbm,
    x_vm, cot_vm, cot_sib, cot_halo, edges, nn, halo, na, nt, w_vm, cp, cph,
    tap_in, tapf, tb, msk, keep, stat, pre, val_s, sig_s, xe, xh, de, dh, dp, dpn,
    tg, tt, g, rd, s1, r2, fs, r3, sf, t_r1, t_s1, t_r2,
    dno, dns, dnr, gx_vm, gin_vm, gtap_vm, fb_s, fb_r, ps_s, ps_r,
    local_sem, w_loc, w_send, w_recv, misc_send, misc_recv, fb_send, fb_recv,
    rd_send, rd_recv, r2_send, r2_recv, r3_send, r3_recv, t_send, t_recv, ps_send, ps_recv,
):
    c = lax.axis_index("dp")
    s = lax.axis_index("seq")
    f = lax.axis_index("fsdp")
    z, y = s // 8, (s // 2) % 4
    x = (s % 2) * 2 + f
    oc = 1 - c

    def dev(core, zz, yy, xx):
        return (core, zz * 8 + yy * 2 + xx // 2, xx % 2)

    def xd(d):
        return (x + d) % 4

    def yd(d):
        return (y + d) % 4

    def zd(d):
        return (z + d) % 4

    nxt, prv = (s + 1) % 32, (s + 31) % 32
    sibling = dev(oc, z, y, x)

    def send(src, dst, send_sem, recv_sem, device):
        pltpu.make_async_remote_copy(
            src_ref=src, dst_ref=dst, send_sem=send_sem, recv_sem=recv_sem,
            device_id=device, device_id_type=MESH,
        ).start()

    partners = [sibling]
    partners += [dev(e, z, y, xd(d)) for d in (1, 2, 3) for e in (0, 1)]
    partners += [dev(c, z, yd(d), x) for d in (1, 2, 3)]
    partners += [dev(c, zd(d), y, x) for d in (1, 2, 3)]
    partners += [(e, q, f) for q in (prv, nxt) for e in (0, 1)]
    partners += [dev(c, zd(d), yd(e), x) for d in (1, 2, 3) for e in (1, 2, 3)]
    barrier = pltpu.get_barrier_semaphore()
    for partner in partners:
        pl.semaphore_signal(barrier, inc=1, device_id=partner, device_id_type=MESH)

    load_x = pltpu.make_async_copy(x_hbm.at[0], x_vm, local_sem.at[0])
    load_cot = pltpu.make_async_copy(cot_hbm.at[0], cot_vm, local_sem.at[1])
    load_cot.start()
    load_x.start()

    def w_columns(j, part):
        return pl.ds(pl.multiple_of(part * D + c * H + j * CH, CH), CH)

    def local_w(j):
        for part in (0, 1):
            pltpu.make_async_copy(
                w_hbm.at[:, w_columns(j, part)],
                w_vm.at[j, pl.ds(pl.multiple_of(f * H, H), H), pl.ds(part * CH, CH)],
                w_loc.at[j],
            ).start()

    def send_w(j):
        for side in (0, 1):
            for part in (0, 1):
                send(
                    w_hbm.at[pl.ds(side * (H // 2), H // 2), w_columns(j, part)],
                    w_vm.at[
                        j,
                        pl.ds(pl.multiple_of(f * H + side * (H // 2), H // 2), H // 2),
                        pl.ds(part * CH, CH),
                    ],
                    w_send.at[j], w_recv.at[j, side], dev(c, z, y, xd(1 if side == 0 else 3)),
                )

    def await_w(j):
        await_bytes(w_vm.at[j, pl.ds(pl.multiple_of(f * H, H), H)], w_loc.at[j])
        for side in (0, 1):
            base = pl.multiple_of((1 - f) * H + side * (H // 2), H // 2)
            await_bytes(w_vm.at[j, pl.ds(base, H // 2)], w_recv.at[j, side])

    for j in range(NC):
        local_w(j)

    frame0 = s * ROWS
    load_cot.wait()
    spoiled = jnp.zeros((ROWS, 128), F32)
    for i in range(D // 128):
        spoiled = spoiled + cot_vm[:, i * 128 : (i + 1) * 128].astype(F32) * 0.0
    local = iota((ROWS, 128), 0)
    bad = jnp.logical_or(spoiled != 0.0, local == poi_ref[0, 0])
    cand = jnp.where(bad, frame0 + local, jnp.int32(BIG))
    cand = jnp.min(cand.reshape(ROWS // 8, 8, 128), axis=0)
    cand = jnp.min(jnp.min(cand, axis=0, keepdims=True), axis=1, keepdims=True)
    row = iota((8, 128), 0)
    tile = jnp.where(row == c, jnp.broadcast_to(cand, (8, 128)), jnp.int32(BIG))
    fb_s[0] = jnp.where(row == 2 + c, len_ref[0], tile)

    pl.semaphore_wait(barrier, len(partners))

    for k, partner in enumerate((sibling, dev(c, z, y, xd(2)), dev(oc, z, y, xd(2)))):
        send(fb_s.at[0], fb_r.at[0, k], fb_send.at[0], fb_recv.at[0], partner)
    send(x_hbm.at[0, pl.ds(ROWS - 32, 32)], edges.at[0], misc_send.at[3], misc_recv.at[3], (c, nxt, f))
    send(x_hbm.at[0, pl.ds(0, 32)], edges.at[1], misc_send.at[3], misc_recv.at[3], (c, prv, f))
    send(
        cot_vm.at[:, pl.ds(pl.multiple_of(oc * H, H), H)], cot_sib,
        misc_send.at[0], misc_recv.at[0], sibling,
    )
    for e in (0, 1):
        cols = pl.ds(e * H, H)
        send(cot_vm.at[pl.ds(ROWS - 16, 16), cols], cot_halo.at[c, 0],
             misc_send.at[1], misc_recv.at[1], (e, nxt, f))
        send(cot_vm.at[pl.ds(0, 16), cols], cot_halo.at[c, 1],
             misc_send.at[1], misc_recv.at[1], (e, prv, f))
    send(taps_ref, tap_in, misc_send.at[2], misc_recv.at[2], dev(c, z, y, xd(3)))
    for j in range(NC):
        send_w(j)

    load_x.wait()

    def normalised(frames):
        xf = frames.astype(F32)
        average = jnp.mean(xf, axis=-1, keepdims=True)
        cent = xf - average
        inverse = lax.rsqrt(jnp.mean(cent * cent, axis=-1, keepdims=True) + 1e-05)
        return (cent * inverse).astype(BF16), average, inverse

    def norm_rows(i, _):
        rows = pl.ds(pl.multiple_of(i * 32, 32), 32)
        nn[rows, :], average, inverse = normalised(x_vm[rows, :])
        stat[0, rows, :] = jnp.broadcast_to(average, (32, 128))
        stat[1, rows, :] = jnp.broadcast_to(inverse, (32, 128))
        return 0

    lax.fori_loop(0, ROWS // 32, norm_rows, 0)

    r0, r1i = iota((ROWS, ROWS), 0), iota((ROWS, ROWS), 1)
    to_phase = one_hot((r0 % 8) * 32 + r0 // 8 == r1i)
    own_rows = pl.ds(pl.multiple_of(c * ROWS, ROWS), ROWS)
    sib_rows = pl.ds(pl.multiple_of(oc * ROWS, ROWS), ROWS)
    na[own_rows, :] = dot(to_phase, nn[...]).astype(BF16)
    send(na.at[own_rows], na.at[own_rows], misc_send.at[4], misc_recv.at[4], sibling)

    await_bytes(fb_r.at[0], fb_recv.at[0])
    fb_s[1] = jnp.minimum(jnp.minimum(fb_s[0], fb_r[0, 0]), jnp.minimum(fb_r[0, 1], fb_r[0, 2]))
    for d in (1, 2, 3):
        send(fb_s.at[1], fb_r.at[1, d - 1], fb_send.at[1], fb_recv.at[1], dev(c, z, yd(d), x))

    for i in range(D // 128):
        cols = pl.ds(i * 128, 128)
        nt[cols, own_rows] = na[own_rows, cols].T

    await_bytes(edges, misc_recv.at[3])
    for side in (0, 1):
        halo[c, side] = normalised(edges[side])[0]
    send(halo.at[c], halo.at[c], misc_send.at[5], misc_recv.at[5], sibling)

    await_bytes(fb_r.at[1], fb_recv.at[1])
    fb_s[2] = jnp.minimum(jnp.minimum(fb_s[1], fb_r[1, 0]), jnp.minimum(fb_r[1, 1], fb_r[1, 2]))
    for d in (1, 2, 3):
        send(fb_s.at[2], fb_r.at[2, d - 1], fb_send.at[2], fb_recv.at[2], dev(c, zd(d), y, x))

    await_bytes(tap_in, misc_recv.at[2])
    mine = jnp.where(f == c, jnp.float32(1.0), jnp.float32(0.0))
    tapf[...] = taps_ref[...].astype(F32) * mine + tap_in[...].astype(F32) * (1.0 - mine)

    await_bytes(na.at[sib_rows], misc_recv.at[4])
    for i in range(D // 128):
        cols = pl.ds(i * 128, 128)
        nt[cols, sib_rows] = na[sib_rows, cols].T
    await_bytes(halo.at[oc], misc_recv.at[5])
    h0, h1 = iota((128, 128), 0), iota((128, 128), 1)
    source = ((h0 % 4) * 32) + ((h0 // 4) % 2) * 16 + h0 // 8
    halo_order = one_hot(source == h1)
    na[512:640, :] = dot(halo_order, halo[...].reshape(128, D)).astype(BF16)

    await_bytes(cot_sib, misc_recv.at[0])
    cp[c] = dot(to_phase, cot_vm[:, pl.ds(pl.multiple_of(c * H, H), H)]).astype(BF16)
    cp[oc] = dot(to_phase, cot_sib[...]).astype(BF16)
    c0, c1 = iota((128, 64), 0), iota((128, 64), 1)
    edge_order = one_hot(
        jnp.logical_and(c0 % 8 < 4, (c0 % 8) * 16 + c0 // 8 == c1)
    )
    await_bytes(cot_halo, misc_recv.at[1])
    cph[...] = dot(edge_order, cot_halo[...].reshape(64, H)).astype(BF16)

    ri = iota((ROWS, 128), 0)
    frame = frame0 + (ri % 8) * 32 + ri // 8
    hr = iota((128, 128), 0)
    place, q = hr % 8, hr // 8
    first_half = jnp.where(place % 2 == 0, q - 16, q + ROWS) + frame0
    halo_frame = jnp.where(place % 2 == 0, q - 32, q + ROWS) + (place // 4) * 16 + frame0

    def valid(flag):
        return jnp.where(flag, jnp.float32(1.0), jnp.float32(0.0))

    def masks(out, limits, edge):
        for u in (0, 1):
            out[u * ROWS : (u + 1) * ROWS, :] = valid(frame < limits[u : u + 1])
        limit = jnp.where((place // 2) % 2 == 0, limits[0:1], limits[1:2])
        out[512:640, :] = valid(jnp.logical_and(edge >= 0, edge < limit))

    masks(msk, fb_s[1, 2:4], halo_frame)

    from_phase = one_hot((r1i % 8) * 32 + r1i // 8 == r0)

    def ring_dev(part, d):
        return dev(c, zd(d), y, x) if part == 0 else dev(c, z, yd(d), x)

    def direct_start(j):
        for part in (0, 1):
            for d in (1, 2, 3):
                src = g.at[j, 0, :, zd(d)] if part == 0 else g.at[j, 1, :, :, yd(d)]
                send(src, rd.at[j, part, d - 1], rd_send.at[j, part], rd_recv.at[j, part], ring_dev(part, d))

    def direct_finish(j):
        for part in (0, 1):
            await_bytes(rd.at[j, part], rd_recv.at[j, part])

            def add(i, _):
                a, b = i // 4, i % 4
                own = g[j, 0, a, z, b] if part == 0 else g[j, 1, a, b, y]
                total = own.astype(F32)
                for d in range(3):
                    total = total + rd[j, part, d, a, b].astype(F32)
                s1[j, part, a, b] = total.astype(BF16)
                return 0

            lax.fori_loop(0, 8, add, 0)
        stage2_start(j)

    def stage2_start(j):
        for d in (1, 2, 3):
            send(s1.at[j, 0, :, yd(d)], r2.at[j, 0, d - 1], r2_send.at[j, 0], r2_recv.at[j, 0],
                 dev(c, z, yd(d), x))
            send(s1.at[j, 1, :, zd(d)], r2.at[j, 1, d - 1], r2_send.at[j, 1], r2_recv.at[j, 1],
                 dev(c, zd(d), y, x))

    def stage2_finish(j):
        for part in (0, 1):
            await_bytes(r2.at[j, part], r2_recv.at[j, part])
            lanes = pl.ds(pl.multiple_of((j % 2) * 256 + part * 128, 128), 128)
            for a in (0, 1):
                total = s1[j, part, a, y if part == 0 else z].astype(F32)
                for d in range(3):
                    total = total + r2[j, part, d, a].astype(F32)
                sf[a, 0:48] = total
                for b in range(4):
                    fs[j // 2, a, b, :, lanes] = sf[a, 12 * b : 12 * b + 16].astype(BF16)

    def stage3_start(q, width):
        for e in (0, 1):
            core = c if e == 0 else oc
            for d in range(4):
                if e == 0 and d == 0:
                    continue
                send(fs.at[q, core, xd(d), :, pl.ds(0, width)], r3.at[q, e, d, :, pl.ds(0, width)],
                     r3_send.at[q, e], r3_recv.at[q, e], dev(core, z, y, xd(d)))

    def stage3_await(q, width, sems):
        await_bytes(r3.at[q, 0, 1:4, :, pl.ds(0, width)], sems.at[q, 0])
        await_bytes(r3.at[q, 1, :, :, pl.ds(0, width)], sems.at[q, 1])

    def stage3_finish(q, width):
        stage3_await(q, width, r3_recv)
        r3[q, 0, 0] = fs[q, c, x]
        squares = jnp.zeros((12, 128), F32)
        for e in (0, 1):
            core = c if e == 0 else oc
            for i in range(4):
                total = r3[q, e, 0, :, i * 128 : (i + 1) * 128].astype(F32)
                for d in range(1, 4):
                    total = total + r3[q, e, d, :, i * 128 : (i + 1) * 128].astype(F32)
                total = total[0:12]
                squares = squares + total * total
                at = pl.multiple_of((i % 2) * D + core * H + (2 * q + i // 2) * CH, CH)
                gin_vm[:, pl.ds(at, CH)] = total
        return squares

    sf[...] = jnp.zeros_like(sf)
    tg[...] = jnp.zeros_like(tg)
    for a in (0, 1):
        for b in range(4):
            fs[2, a, b, :, 512:640] = jnp.zeros((16, 128), BF16)

    sub = iota((16, 8, 128), 1)

    def chunk(j, _):
        lanes = pl.ds(pl.multiple_of(j * CH, CH), CH)
        for k in range(KT):
            tb[k] = jnp.broadcast_to(tapf[k : k + 1, lanes], (8, 128))
        await_w(j)
        pre[...] = dot(na[...], w_vm[j])

        def gated(rows):
            sig = sigmoid(pre[rows, CH:])
            val = pre[rows, :CH]
            return val, sig, val * sig * msk[rows, :]

        main = []
        for u in (0, 1):
            rows = slice(u * ROWS, (u + 1) * ROWS)
            val, sig, glued = gated(rows)
            val_s[rows, :] = val
            sig_s[rows, :] = sig
            xe[u, 16:48] = glued.reshape(32, 8, CH)
        h3 = gated(slice(512, 640))[2].reshape(16, 8, CH)
        h4 = pltpu.roll(h3, 4, 1)
        for u in (0, 1):
            left = h4 if u == 0 else pltpu.roll(h3, 2, 1)
            xe[u, 0:16] = jnp.where(sub == 0, left, pltpu.roll(xe[u, 32:48], 1, 1))
            xe[u, 48:64] = jnp.where(
                sub == 7, pltpu.roll(h3, 6 - 2 * u, 1), pltpu.roll(xe[u, 16:32], 7, 1)
            )
        xh[0:16] = jnp.where(
            sub == 1, pltpu.roll(xe[0, 32:48], 2, 1),
            jnp.where(sub == 3, pltpu.roll(xe[1, 32:48], 4, 1), h3),
        )
        xh[16:32] = jnp.where(sub % 2 == 0, h4, h3)
        xh[32:48] = jnp.where(
            sub == 0, xe[0, 16:32], jnp.where(sub == 2, pltpu.roll(xe[1, 16:32], 2, 1), h4)
        )

        def conv(window):
            total = tb[0][None] * window[0:8]
            for k in range(1, KT):
                total = total + tb[k][None] * window[k : k + 8]
            return total

        def through_swish(total, cot):
            gate = sigmoid(total)
            return cot * gate * (1.0 + total * (1.0 - gate))

        def forward(i, _):
            u, b = i // 4, i % 4
            total = conv(xe[u, pl.ds(b * 8, 39)])
            cot = cp[u, pl.ds(pl.multiple_of(b * 64, 64), 64), lanes].astype(F32)
            cot = cot * keep[pl.ds(pl.multiple_of(i * 64, 64), 64), :]
            de[u, pl.ds(16 + b * 8, 8)] = through_swish(total, cot.reshape(8, 8, CH))
            return 0

        @pl.when(j == 0)
        def _():
            await_bytes(fb_r.at[2], fb_recv.at[2])
            votes = jnp.minimum(
                jnp.minimum(fb_s[2], fb_r[2, 0]), jnp.minimum(fb_r[2, 1], fb_r[2, 2])
            )
            masks(keep, votes, first_half)

        lax.fori_loop(0, 8, forward, 0, unroll=4)

        def forward_edge(b, _):
            total = conv(xh[pl.ds(b * 8, 39)])
            cot = cph[pl.ds(pl.multiple_of(b * 64, 64), 64), lanes].astype(F32)
            cot = cot * keep[pl.ds(pl.multiple_of(512 + b * 64, 64), 64), :]
            dh[pl.ds(b * 8, 8)] = through_swish(total, cot.reshape(8, 8, CH))
            return 0

        lax.fori_loop(0, 2, forward_edge, 0)
        d3 = dh[...]
        for u in (0, 1):
            left = d3 if u == 0 else pltpu.roll(d3, 6, 1)
            de[u, 0:16] = jnp.where(sub == 0, left, pltpu.roll(de[u, 32:48], 1, 1))
            de[u, 48:64] = jnp.where(
                sub == 7, pltpu.roll(d3, 6 - 2 * u, 1), pltpu.roll(de[u, 16:32], 7, 1)
            )

        def backward(i, _):
            u, b = i // 4, i % 4
            window = de[u, pl.ds(b * 8 + 1, 39)]
            total = tb[0][None] * window[31:39]
            for k in range(1, KT):
                total = total + tb[k][None] * window[31 - k : 39 - k]
            rows = pl.ds(pl.multiple_of(i * 64, 64), 64)
            dglued = total.reshape(64, CH) * msk[rows, :]
            val, sig = val_s[rows, :], sig_s[rows, :]
            dval = dglued * sig
            dp[rows, 0:CH] = dval.astype(BF16)
            dp[rows, CH:] = (dval * val * (1.0 - sig)).astype(BF16)
            return 0

        lax.fori_loop(0, 8, backward, 0, unroll=4)

        for i in range(8):
            grad = dot(nt[i * 192 : (i + 1) * 192, :], dp[...])
            for part in (0, 1):
                half = grad[:, part * CH : (part + 1) * CH].astype(BF16)
                g[j, part, i // 4, i % 4] = half.reshape(4, 48, CH)

        direct_start(j)

        for h in (0, 16):

            def tap_terms(i, total):
                u, b = i // 4, i % 4
                window = xe[u, pl.ds(b * 8 + h, 23)]
                grads = de[u, pl.ds(16 + b * 8, 8)]
                for m in range(8):
                    total = total + grads[m][None] * window[m : m + 16]
                return total

            terms = lax.fori_loop(0, 8, tap_terms, jnp.zeros((16, 8, CH), F32), unroll=4)
            tg[j, h : h + 16] = jnp.sum(terms, axis=1)
        for u in (0, 1):
            rows = slice(u * ROWS, (u + 1) * ROWS)
            dpn[j, rows, :] = dot(from_phase, dp[rows, :]).astype(BF16)

        @pl.when(j >= 1)
        def _():
            direct_finish(j - 1)

        @pl.when(j >= 2)
        def _():
            stage2_finish(j - 2)

        @pl.when(jnp.logical_and(j >= 3, j % 2 == 1))
        def _():
            stage3_start((j - 3) // 2, 512)

        return 0

    lax.fori_loop(0, NC, chunk, 0)

    for j in range(NC):
        tt[j * CH : (j + 1) * CH, :] = tg[j].T.astype(BF16)
    for d in (1, 2, 3):
        send(tt.at[pl.ds(pl.multiple_of(zd(d) * 192, 16), 192)], t_r1.at[d - 1],
             t_send.at[0], t_recv.at[0], dev(c, zd(d), y, x))

    dims = (((1,), (1,)), ((), ()))

    def dnormed(u, cols):
        rows = pl.ds(pl.multiple_of(u * ROWS, ROWS), ROWS)
        total = dot(dpn[0, rows, :], w_vm[0, cols, :], dims)
        for j in range(1, NC):
            total = total + dot(dpn[j, rows, :], w_vm[j, cols, :], dims)
        return total

    def sibling_part(i, _):
        cols = pl.ds(pl.multiple_of(i * 256, 256), 256)
        dns[:, cols] = dnormed(oc, cols).astype(BF16)
        return 0

    lax.fori_loop(0, D // 256, sibling_part, 0)
    send(dns, dnr, misc_send.at[6], misc_recv.at[6], sibling)

    direct_finish(NC - 1)
    stage2_finish(NC - 2)
    await_bytes(t_r1, t_recv.at[0])
    mine = tt[pl.ds(pl.multiple_of(z * 192, 16), 192), :].astype(F32)
    for d in range(3):
        mine = mine + t_r1[d].astype(F32)
    t_s1[...] = mine.astype(BF16)
    for d in (1, 2, 3):
        send(t_s1.at[pl.ds(pl.multiple_of(yd(d) * 48, 16), 48)], t_r2.at[d - 1],
             t_send.at[1], t_recv.at[1], dev(c, z, yd(d), x))

    def own_part(i, _):
        cols = pl.ds(pl.multiple_of(i * 256, 256), 256)
        dno[:, cols] = dnormed(c, cols)
        return 0

    lax.fori_loop(0, D // 256, own_part, 0)

    stage2_finish(NC - 1)
    await_bytes(t_r2, t_recv.at[1])
    mine = t_s1[pl.ds(pl.multiple_of(y * 48, 16), 48), :].astype(F32)
    for d in range(3):
        mine = mine + t_r2[d].astype(F32)
    sf[0, 0:48] = mine
    for b in range(4):
        fs[2, c, b, :, 512:640] = sf[0, 12 * b : 12 * b + 16].astype(BF16)

    stage3_start(2, 640)

    await_bytes(dnr, misc_recv.at[6])

    def input_rows(i, _):
        rows = pl.ds(pl.multiple_of(i * 32, 32), 32)
        average, inverse = stat[0, rows, 0:1], stat[1, rows, 0:1]
        xhat = (x_vm[rows, :].astype(F32) - average) * inverse
        grad = dno[rows, :] + dnr[rows, :].astype(F32)
        m1 = jnp.mean(grad, axis=-1, keepdims=True)
        m2 = jnp.mean(grad * xhat, axis=-1, keepdims=True)
        gx_vm[rows, :] = (inverse * (grad - m1 - xhat * m2)).astype(BF16)
        return 0

    lax.fori_loop(0, ROWS // 32, input_rows, 0)
    store_gx = pltpu.make_async_copy(gx_vm, gx_hbm.at[0], local_sem.at[0])
    store_gx.start()

    squares = stage3_finish(0, 512) + stage3_finish(1, 512) + stage3_finish(2, 640)
    total = r3[2, 0, 0, :, 512:640].astype(F32)
    for d in range(1, 4):
        total = total + r3[2, 0, d, :, 512:640].astype(F32)
    tap_rows = total[0:12]
    squares = squares + tap_rows * tap_rows

    part = jnp.sum(jnp.sum(squares, axis=0, keepdims=True), axis=1, keepdims=True)
    ps_s[0] = jnp.broadcast_to(part, (8, 128))
    count = 0
    for e in (0, 1):
        for d in range(4):
            if e == 0 and d == 0:
                continue
            send(ps_s.at[0], ps_r.at[count], ps_send.at[0], ps_recv.at[0],
                 dev(c if e == 0 else oc, z, y, xd(d)))
            count += 1
    await_bytes(ps_r.at[0:7], ps_recv.at[0])
    total = ps_s[0]
    for i in range(7):
        total = total + ps_r[i]
    ps_s[1] = total
    count = 7
    for d in range(4):
        for e in range(4):
            if d == 0 and e == 0:
                continue
            send(ps_s.at[1], ps_r.at[count], ps_send.at[1], ps_recv.at[1], dev(c, zd(d), yd(e), x))
            count += 1
    await_bytes(ps_r.at[7:22], ps_recv.at[1])
    total = ps_s[1]
    for i in range(7, 22):
        total = total + ps_r[i]
    msq = total[0:1, 0:1] / jnp.float32(2 * D * D + D * KT)
    scale = 1.0 / jnp.maximum(jnp.float32(1.0), jnp.sqrt(msq))
    gin_vm[...] = gin_vm[...] * scale
    gtap_vm[...] = (tap_rows * scale)[:, 0:KT]
    store_gin = pltpu.make_async_copy(gin_vm, gin_hbm, local_sem.at[1])
    store_gin.start()
    store_gtap = pltpu.make_async_copy(gtap_vm, gtap_hbm, local_sem.at[2])
    store_gtap.start()

    for j in range(NC):
        await_bytes(w_vm.at[j, pl.ds(0, H)], w_send.at[j])
        for part in (0, 1):
            await_bytes(r2.at[j, part], r2_send.at[j, part])
    for j in range(NC):
        for part in (0, 1):
            await_bytes(rd.at[j, part], rd_send.at[j, part])
    await_bytes(cot_sib, misc_send.at[0])
    await_bytes(cot_halo, misc_send.at[1])
    await_bytes(tap_in, misc_send.at[2])
    await_bytes(edges, misc_send.at[3])
    await_bytes(na.at[own_rows], misc_send.at[4])
    await_bytes(halo.at[c], misc_send.at[5])
    await_bytes(dns, misc_send.at[6])
    for i in range(3):
        await_bytes(fb_r.at[i], fb_send.at[i])
    for q, width in ((0, 512), (1, 512), (2, 640)):
        stage3_await(q, width, r3_send)
    await_bytes(t_r1, t_send.at[0])
    await_bytes(t_r2, t_send.at[1])
    await_bytes(ps_r.at[0:7], ps_send.at[0])
    await_bytes(ps_r.at[7:22], ps_send.at[1])
    store_gx.wait()
    store_gin.wait()
    store_gtap.wait()


def hand_over(gx, gin, gtap, gx_out, gin_out, gtap_out):
    gx_out[...] = gx[...]
    gin_out[...] = gin[...]
    gtap_out[...] = gtap[...]


def body(activations, cotangent, lengths, poison, w_in, taps):
    vmem = pltpu.VMEM
    dma = pltpu.SemaphoreType.DMA
    scratch = [
        vmem((ROWS, D), BF16),
        vmem((ROWS, D), BF16),
        vmem((ROWS, H), BF16),
        vmem((2, 2, 16, H), BF16),
        vmem((2, 32, D), BF16),
        vmem((ROWS, D), BF16),
        vmem((2, 2, 32, D), BF16),
        vmem((640, D), BF16),
        vmem((D, 512), BF16),
        vmem((NC, D, 2 * CH), BF16),
        vmem((2, ROWS, H), BF16),
        vmem((128, H), BF16),
        vmem((KT, H), BF16),
        vmem((KT, H), F32),
        vmem((KT, 8, CH), F32),
        vmem((640, 128), F32),
        vmem((640, 128), F32),
        vmem((2, ROWS, 128), F32),
        vmem((640, 2 * CH), F32),
        vmem((512, CH), F32),
        vmem((512, CH), F32),
        vmem((2, 64, 8, CH), F32),
        vmem((48, 8, CH), F32),
        vmem((2, 64, 8, CH), F32),
        vmem((16, 8, CH), F32),
        vmem((512, 2 * CH), BF16),
        vmem((NC, 512, 2 * CH), BF16),
        vmem((NC, 128, CH), F32),
        vmem((H, 128), BF16),
        vmem((NC, 2, 2, 4, 4, 48, CH), BF16),
        vmem((NC, 2, 3, 2, 4, 48, CH), BF16),
        vmem((NC, 2, 2, 4, 48, CH), BF16),
        vmem((NC, 2, 3, 2, 48, CH), BF16),
        vmem((3, 2, 4, 16, 640), BF16),
        vmem((3, 2, 4, 16, 640), BF16),
        vmem((2, 56, CH), F32),
        vmem((3, 192, 128), BF16),
        vmem((192, 128), BF16),
        vmem((3, 48, 128), BF16),
        vmem((ROWS, D), F32),
        vmem((ROWS, D), BF16),
        vmem((ROWS, D), BF16),
        vmem((ROWS, D), BF16),
        vmem((12, 2 * D), F32),
        vmem((12, KT), F32),
        vmem((3, 8, 128), jnp.int32),
        vmem((3, 3, 8, 128), jnp.int32),
        vmem((2, 8, 128), F32),
        vmem((22, 8, 128), F32),
        dma((3,)),
        dma((NC,)), dma((NC,)), dma((NC, 2)),
        dma((7,)), dma((7,)),
        dma((3,)), dma((3,)),
        dma((NC, 2)), dma((NC, 2)),
        dma((NC, 2)), dma((NC, 2)),
        dma((3, 2)), dma((3, 2)),
        dma((2,)), dma((2,)),
        dma((2,)), dma((2,)),
    ]
    anywhere = pl.BlockSpec(memory_space=pl.ANY)
    in_vmem = pl.BlockSpec(memory_space=pltpu.VMEM)
    in_smem = pl.BlockSpec(memory_space=pltpu.SMEM)
    shapes = (
        jax.ShapeDtypeStruct((1, ROWS, D), BF16),
        jax.ShapeDtypeStruct((12, 2 * D), F32),
        jax.ShapeDtypeStruct((12, KT), F32),
    )
    results = pl.pallas_call(
        kernel,
        out_shape=shapes,
        in_specs=[in_smem, in_smem, in_vmem, anywhere, anywhere, anywhere],
        out_specs=(anywhere, anywhere, anywhere),
        scratch_shapes=scratch,
        compiler_params=pltpu.CompilerParams(
            collective_id=0, has_side_effects=True, vmem_limit_bytes=56 * 1024 * 1024
        ),
        name="conformer_conv",
    )(lengths, poison, taps.T, activations, cotangent, w_in)
    return pl.pallas_call(
        hand_over,
        out_shape=shapes,
        in_specs=[in_vmem] * 3,
        out_specs=(in_vmem,) * 3,
        name="hand_over",
    )(*results)


def solution(mesh):
    placed = (
        P(("dp", "fsdp"), "seq", None),
        P(("dp", "fsdp"), "seq", None),
        P(("dp", "fsdp")),
        P(("dp", "fsdp"), "seq"),
        P("fsdp", None),
        P("fsdp", None),
    )
    return jax.shard_map(
        body,
        mesh=mesh,
        in_specs=placed,
        out_specs=(
            P(("dp", "fsdp"), "seq", None),
            P(("dp", "seq", "fsdp"), None),
            P(("dp", "seq", "fsdp"), None),
        ),
        check_vma=False,
    )
```

```python
import functools

import jax
import jax.numpy as jnp
from jax import lax
from jax.experimental import pallas as pl
from jax.experimental.pallas import tpu as pltpu
from jax.sharding import PartitionSpec as P

MESH = pl.DeviceIdType.MESH
F32 = jnp.float32
BF16 = jnp.bfloat16

D = 1536
H = 768
KT = 32
ROWS = 256
FRAMES = 8192
NC = 6
CH = 128
BIG = FRAMES


def sigmoid(v):
    return 0.5 * jnp.tanh(0.5 * v) + 0.5


def dot(a, b, dims=(((1,), (0,)), ((), ()))):
    return lax.dot_general(a, b, dims, preferred_element_type=F32)


def iota(shape, dim):
    return lax.broadcasted_iota(jnp.int32, shape, dim)


def one_hot(flag):
    return jnp.where(flag, jnp.float32(1.0), jnp.float32(0.0)).astype(BF16)


def await_bytes(ref, sem):
    pltpu.make_async_copy(ref, ref, sem).wait()


def kernel(
    len_ref, poi_ref, taps_ref, x_hbm, cot_hbm, w_hbm,
    gx_hbm, gin_hbm, gtap_hbm,
    x_vm, cot_vm, cot_sib, cot_halo, edges, nn, halo, na, nt, w_vm, cp, cph,
    tap_in, tapf, tb, msk, keep, stat, pre, val_s, sig_s, xe, xh, de, dh, dp, dpn,
    tg, tt, g, rd, s1, r2, fs, r3, sf, t_r1, t_s1, t_r2,
    dno, dns, dnr, gx_vm, gin_vm, gtap_vm, fb_s, fb_r, ps_s, ps_r,
    local_sem, w_loc, w_send, w_recv, misc_send, misc_recv, fb_send, fb_recv,
    rd_send, rd_recv, r2_send, r2_recv, r3_send, r3_recv, t_send, t_recv, ps_send, ps_recv,
):
    c = lax.axis_index("dp")
    s = lax.axis_index("seq")
    f = lax.axis_index("fsdp")
    z, y = s // 8, (s // 2) % 4
    x = (s % 2) * 2 + f
    oc = 1 - c

    def dev(core, zz, yy, xx):
        return (core, zz * 8 + yy * 2 + xx // 2, xx % 2)

    def xd(d):
        return (x + d) % 4

    def yd(d):
        return (y + d) % 4

    def zd(d):
        return (z + d) % 4

    nxt, prv = (s + 1) % 32, (s + 31) % 32
    sibling = dev(oc, z, y, x)

    def send(src, dst, send_sem, recv_sem, device):
        pltpu.make_async_remote_copy(
            src_ref=src, dst_ref=dst, send_sem=send_sem, recv_sem=recv_sem,
            device_id=device, device_id_type=MESH,
        ).start()

    partners = [sibling]
    partners += [dev(e, z, y, xd(d)) for d in (1, 2, 3) for e in (0, 1)]
    partners += [dev(c, z, yd(d), x) for d in (1, 2, 3)]
    partners += [dev(c, zd(d), y, x) for d in (1, 2, 3)]
    partners += [(e, q, f) for q in (prv, nxt) for e in (0, 1)]
    partners += [dev(c, zd(d), yd(e), x) for d in (1, 2, 3) for e in (1, 2, 3)]
    barrier = pltpu.get_barrier_semaphore()
    for partner in partners:
        pl.semaphore_signal(barrier, inc=1, device_id=partner, device_id_type=MESH)

    load_x = pltpu.make_async_copy(x_hbm.at[0], x_vm, local_sem.at[0])
    load_cot = pltpu.make_async_copy(cot_hbm.at[0], cot_vm, local_sem.at[1])
    load_cot.start()
    load_x.start()

    def w_columns(j, part):
        return pl.ds(pl.multiple_of(part * D + c * H + j * CH, CH), CH)

    def local_w(j):
        for part in (0, 1):
            pltpu.make_async_copy(
                w_hbm.at[:, w_columns(j, part)],
                w_vm.at[j, pl.ds(pl.multiple_of(f * H, H), H), pl.ds(part * CH, CH)],
                w_loc.at[j],
            ).start()

    def send_w(j):
        for side in (0, 1):
            for part in (0, 1):
                send(
                    w_hbm.at[pl.ds(side * (H // 2), H // 2), w_columns(j, part)],
                    w_vm.at[
                        j,
                        pl.ds(pl.multiple_of(f * H + side * (H // 2), H // 2), H // 2),
                        pl.ds(part * CH, CH),
                    ],
                    w_send.at[j], w_recv.at[j, side], dev(c, z, y, xd(1 if side == 0 else 3)),
                )

    def await_w(j):
        await_bytes(w_vm.at[j, pl.ds(pl.multiple_of(f * H, H), H)], w_loc.at[j])
        for side in (0, 1):
            base = pl.multiple_of((1 - f) * H + side * (H // 2), H // 2)
            await_bytes(w_vm.at[j, pl.ds(base, H // 2)], w_recv.at[j, side])

    for j in range(NC):
        local_w(j)

    frame0 = s * ROWS
    load_cot.wait()
    spoiled = jnp.zeros((ROWS, 128), F32)
    for i in range(D // 128):
        spoiled = spoiled + cot_vm[:, i * 128 : (i + 1) * 128].astype(F32) * 0.0
    local = iota((ROWS, 128), 0)
    bad = jnp.logical_or(spoiled != 0.0, local == poi_ref[0, 0])
    cand = jnp.where(bad, frame0 + local, jnp.int32(BIG))
    cand = jnp.min(cand.reshape(ROWS // 8, 8, 128), axis=0)
    cand = jnp.min(jnp.min(cand, axis=0, keepdims=True), axis=1, keepdims=True)
    row = iota((8, 128), 0)
    tile = jnp.where(row == c, jnp.broadcast_to(cand, (8, 128)), jnp.int32(BIG))
    fb_s[0] = jnp.where(row == 2 + c, len_ref[0], tile)

    pl.semaphore_wait(barrier, len(partners))

    for k, partner in enumerate((sibling, dev(c, z, y, xd(2)), dev(oc, z, y, xd(2)))):
        send(fb_s.at[0], fb_r.at[0, k], fb_send.at[0], fb_recv.at[0], partner)
    send(x_hbm.at[0, pl.ds(ROWS - 32, 32)], edges.at[0], misc_send.at[3], misc_recv.at[3], (c, nxt, f))
    send(x_hbm.at[0, pl.ds(0, 32)], edges.at[1], misc_send.at[3], misc_recv.at[3], (c, prv, f))
    send(
        cot_vm.at[:, pl.ds(pl.multiple_of(oc * H, H), H)], cot_sib,
        misc_send.at[0], misc_recv.at[0], sibling,
    )
    for e in (0, 1):
        cols = pl.ds(e * H, H)
        send(cot_vm.at[pl.ds(ROWS - 16, 16), cols], cot_halo.at[c, 0],
             misc_send.at[1], misc_recv.at[1], (e, nxt, f))
        send(cot_vm.at[pl.ds(0, 16), cols], cot_halo.at[c, 1],
             misc_send.at[1], misc_recv.at[1], (e, prv, f))
    send(taps_ref, tap_in, misc_send.at[2], misc_recv.at[2], dev(c, z, y, xd(3)))
    for j in range(NC):
        send_w(j)

    load_x.wait()

    def normalised(frames):
        xf = frames.astype(F32)
        average = jnp.mean(xf, axis=-1, keepdims=True)
        cent = xf - average
        inverse = lax.rsqrt(jnp.mean(cent * cent, axis=-1, keepdims=True) + 1e-05)
        return (cent * inverse).astype(BF16), average, inverse

    def norm_rows(i, _):
        rows = pl.ds(pl.multiple_of(i * 32, 32), 32)
        nn[rows, :], average, inverse = normalised(x_vm[rows, :])
        stat[0, rows, :] = jnp.broadcast_to(average, (32, 128))
        stat[1, rows, :] = jnp.broadcast_to(inverse, (32, 128))
        return 0

    lax.fori_loop(0, ROWS // 32, norm_rows, 0)

    r0, r1i = iota((ROWS, ROWS), 0), iota((ROWS, ROWS), 1)
    to_phase = one_hot((r0 % 8) * 32 + r0 // 8 == r1i)
    own_rows = pl.ds(pl.multiple_of(c * ROWS, ROWS), ROWS)
    sib_rows = pl.ds(pl.multiple_of(oc * ROWS, ROWS), ROWS)
    na[own_rows, :] = dot(to_phase, nn[...]).astype(BF16)
    send(na.at[own_rows], na.at[own_rows], misc_send.at[4], misc_recv.at[4], sibling)

    await_bytes(fb_r.at[0, 0:3], fb_recv.at[0])
    fb_s[1] = jnp.minimum(jnp.minimum(fb_s[0], fb_r[0, 0]), jnp.minimum(fb_r[0, 1], fb_r[0, 2]))
    for i in range(1, 16):
        send(fb_s.at[1], fb_r.at[1, i - 1], fb_send.at[1], fb_recv.at[1], dev(c, zd(i // 4), yd(i % 4), x))

    for i in range(D // 128):
        cols = pl.ds(i * 128, 128)
        nt[cols, own_rows] = na[own_rows, cols].T

    await_bytes(edges, misc_recv.at[3])
    for side in (0, 1):
        halo[c, side] = normalised(edges[side])[0]
    send(halo.at[c], halo.at[c], misc_send.at[5], misc_recv.at[5], sibling)

    await_bytes(tap_in, misc_recv.at[2])
    mine = jnp.where(f == c, jnp.float32(1.0), jnp.float32(0.0))
    tapf[...] = taps_ref[...].astype(F32) * mine + tap_in[...].astype(F32) * (1.0 - mine)

    await_bytes(na.at[sib_rows], misc_recv.at[4])
    for i in range(D // 128):
        cols = pl.ds(i * 128, 128)
        nt[cols, sib_rows] = na[sib_rows, cols].T
    await_bytes(halo.at[oc], misc_recv.at[5])
    h0, h1 = iota((128, 128), 0), iota((128, 128), 1)
    source = ((h0 % 4) * 32) + ((h0 // 4) % 2) * 16 + h0 // 8
    halo_order = one_hot(source == h1)
    na[512:640, :] = dot(halo_order, halo[...].reshape(128, D)).astype(BF16)

    await_bytes(cot_sib, misc_recv.at[0])
    cp[c] = dot(to_phase, cot_vm[:, pl.ds(pl.multiple_of(c * H, H), H)]).astype(BF16)
    cp[oc] = dot(to_phase, cot_sib[...]).astype(BF16)
    c0, c1 = iota((128, 64), 0), iota((128, 64), 1)
    edge_order = one_hot(
        jnp.logical_and(c0 % 8 < 4, (c0 % 8) * 16 + c0 // 8 == c1)
    )
    await_bytes(cot_halo, misc_recv.at[1])
    cph[...] = dot(edge_order, cot_halo[...].reshape(64, H)).astype(BF16)

    ri = iota((ROWS, 128), 0)
    frame = frame0 + (ri % 8) * 32 + ri // 8
    hr = iota((128, 128), 0)
    place, q = hr % 8, hr // 8
    first_half = jnp.where(place % 2 == 0, q - 16, q + ROWS) + frame0
    halo_frame = jnp.where(place % 2 == 0, q - 32, q + ROWS) + (place // 4) * 16 + frame0

    def valid(flag):
        return jnp.where(flag, jnp.float32(1.0), jnp.float32(0.0))

    def masks(out, limits, edge):
        for u in (0, 1):
            out[u * ROWS : (u + 1) * ROWS, :] = valid(frame < limits[u : u + 1])
        limit = jnp.where((place // 2) % 2 == 0, limits[0:1], limits[1:2])
        out[512:640, :] = valid(jnp.logical_and(edge >= 0, edge < limit))

    masks(msk, fb_s[1, 2:4], halo_frame)

    from_phase = one_hot((r1i % 8) * 32 + r1i // 8 == r0)

    def ring_dev(part, d):
        return dev(c, zd(d), y, x) if part == 0 else dev(c, z, yd(d), x)

    def direct_start(j):
        for part in (0, 1):
            for d in (1, 2, 3):
                src = g.at[j, 0, :, zd(d)] if part == 0 else g.at[j, 1, :, :, yd(d)]
                send(src, rd.at[j, part, d - 1], rd_send.at[j, part], rd_recv.at[j, part], ring_dev(part, d))

    def direct_finish(j):
        for part in (0, 1):
            await_bytes(rd.at[j, part], rd_recv.at[j, part])

            def add(i, _):
                a, b = i // 4, i % 4
                own = g[j, 0, a, z, b] if part == 0 else g[j, 1, a, b, y]
                total = own.astype(F32)
                for d in range(3):
                    total = total + rd[j, part, d, a, b].astype(F32)
                s1[j, part, a, b] = total.astype(BF16)
                return 0

            lax.fori_loop(0, 8, add, 0)
        stage2_start(j)

    def stage2_start(j):
        for d in (1, 2, 3):
            send(s1.at[j, 0, :, yd(d)], r2.at[j, 0, d - 1], r2_send.at[j, 0], r2_recv.at[j, 0],
                 dev(c, z, yd(d), x))
            send(s1.at[j, 1, :, zd(d)], r2.at[j, 1, d - 1], r2_send.at[j, 1], r2_recv.at[j, 1],
                 dev(c, zd(d), y, x))

    def stage2_finish(j):
        for part in (0, 1):
            await_bytes(r2.at[j, part], r2_recv.at[j, part])
            lanes = pl.ds(pl.multiple_of((j % 2) * 256 + part * 128, 128), 128)
            for a in (0, 1):
                total = s1[j, part, a, y if part == 0 else z].astype(F32)
                for d in range(3):
                    total = total + r2[j, part, d, a].astype(F32)
                sf[a, 0:48] = total
                for b in range(4):
                    fs[j // 2, a, b, :, lanes] = sf[a, 12 * b : 12 * b + 16].astype(BF16)

    def stage3_start(q, width):
        for e in (0, 1):
            core = c if e == 0 else oc
            for d in range(4):
                if e == 0 and d == 0:
                    continue
                send(fs.at[q, core, xd(d), :, pl.ds(0, width)], r3.at[q, e, d, :, pl.ds(0, width)],
                     r3_send.at[q, e], r3_recv.at[q, e], dev(core, z, y, xd(d)))

    def stage3_await(q, width, sems):
        await_bytes(r3.at[q, 0, 1:4, :, pl.ds(0, width)], sems.at[q, 0])
        await_bytes(r3.at[q, 1, :, :, pl.ds(0, width)], sems.at[q, 1])

    def stage3_finish(q, width):
        stage3_await(q, width, r3_recv)
        r3[q, 0, 0] = fs[q, c, x]
        squares = jnp.zeros((12, 128), F32)
        for e in (0, 1):
            core = c if e == 0 else oc
            for i in range(4):
                total = r3[q, e, 0, :, i * 128 : (i + 1) * 128].astype(F32)
                for d in range(1, 4):
                    total = total + r3[q, e, d, :, i * 128 : (i + 1) * 128].astype(F32)
                total = total[0:12]
                squares = squares + total * total
                at = pl.multiple_of((i % 2) * D + core * H + (2 * q + i // 2) * CH, CH)
                gin_vm[:, pl.ds(at, CH)] = total
        return squares

    sf[...] = jnp.zeros_like(sf)
    tg[...] = jnp.zeros_like(tg)
    for a in (0, 1):
        for b in range(4):
            fs[2, a, b, :, 512:640] = jnp.zeros((16, 128), BF16)

    sub = iota((16, 8, 128), 1)

    def chunk(j, _):
        lanes = pl.ds(pl.multiple_of(j * CH, CH), CH)
        for k in range(KT):
            tb[k] = jnp.broadcast_to(tapf[k : k + 1, lanes], (8, 128))
        await_w(j)
        pre[...] = dot(na[...], w_vm[j])

        def gated(rows):
            sig = sigmoid(pre[rows, CH:])
            val = pre[rows, :CH]
            return val, sig, val * sig * msk[rows, :]

        main = []
        for u in (0, 1):
            rows = slice(u * ROWS, (u + 1) * ROWS)
            val, sig, glued = gated(rows)
            val_s[rows, :] = val
            sig_s[rows, :] = sig
            xe[u, 16:48] = glued.reshape(32, 8, CH)
        h3 = gated(slice(512, 640))[2].reshape(16, 8, CH)
        h4 = pltpu.roll(h3, 4, 1)
        for u in (0, 1):
            left = h4 if u == 0 else pltpu.roll(h3, 2, 1)
            xe[u, 0:16] = jnp.where(sub == 0, left, pltpu.roll(xe[u, 32:48], 1, 1))
            xe[u, 48:64] = jnp.where(
                sub == 7, pltpu.roll(h3, 6 - 2 * u, 1), pltpu.roll(xe[u, 16:32], 7, 1)
            )
        xh[0:16] = jnp.where(
            sub == 1, pltpu.roll(xe[0, 32:48], 2, 1),
            jnp.where(sub == 3, pltpu.roll(xe[1, 32:48], 4, 1), h3),
        )
        xh[16:32] = jnp.where(sub % 2 == 0, h4, h3)
        xh[32:48] = jnp.where(
            sub == 0, xe[0, 16:32], jnp.where(sub == 2, pltpu.roll(xe[1, 16:32], 2, 1), h4)
        )

        def conv(window):
            total = tb[0][None] * window[0:8]
            for k in range(1, KT):
                total = total + tb[k][None] * window[k : k + 8]
            return total

        def through_swish(total, cot):
            gate = sigmoid(total)
            return cot * gate * (1.0 + total * (1.0 - gate))

        def forward(i, _):
            u, b = i // 4, i % 4
            total = conv(xe[u, pl.ds(b * 8, 39)])
            cot = cp[u, pl.ds(pl.multiple_of(b * 64, 64), 64), lanes].astype(F32)
            cot = cot * keep[pl.ds(pl.multiple_of(i * 64, 64), 64), :]
            de[u, pl.ds(16 + b * 8, 8)] = through_swish(total, cot.reshape(8, 8, CH))
            return 0

        @pl.when(j == 0)
        def _():
            await_bytes(fb_r.at[1], fb_recv.at[1])
            votes = fb_s[1]
            for i in range(15):
                votes = jnp.minimum(votes, fb_r[1, i])
            masks(keep, votes, first_half)

        lax.fori_loop(0, 8, forward, 0, unroll=4)

        def forward_edge(b, _):
            total = conv(xh[pl.ds(b * 8, 39)])
            cot = cph[pl.ds(pl.multiple_of(b * 64, 64), 64), lanes].astype(F32)
            cot = cot * keep[pl.ds(pl.multiple_of(512 + b * 64, 64), 64), :]
            dh[pl.ds(b * 8, 8)] = through_swish(total, cot.reshape(8, 8, CH))
            return 0

        lax.fori_loop(0, 2, forward_edge, 0)
        d3 = dh[...]
        for u in (0, 1):
            left = d3 if u == 0 else pltpu.roll(d3, 6, 1)
            de[u, 0:16] = jnp.where(sub == 0, left, pltpu.roll(de[u, 32:48], 1, 1))
            de[u, 48:64] = jnp.where(
                sub == 7, pltpu.roll(d3, 6 - 2 * u, 1), pltpu.roll(de[u, 16:32], 7, 1)
            )

        def backward(i, _):
            u, b = i // 4, i % 4
            window = de[u, pl.ds(b * 8 + 1, 39)]
            total = tb[0][None] * window[31:39]
            for k in range(1, KT):
                total = total + tb[k][None] * window[31 - k : 39 - k]
            rows = pl.ds(pl.multiple_of(i * 64, 64), 64)
            dglued = total.reshape(64, CH) * msk[rows, :]
            val, sig = val_s[rows, :], sig_s[rows, :]
            dval = dglued * sig
            dp[rows, 0:CH] = dval.astype(BF16)
            dp[rows, CH:] = (dval * val * (1.0 - sig)).astype(BF16)
            return 0

        lax.fori_loop(0, 8, backward, 0, unroll=4)

        for i in range(8):
            grad = dot(nt[i * 192 : (i + 1) * 192, :], dp[...])
            for part in (0, 1):
                half = grad[:, part * CH : (part + 1) * CH].astype(BF16)
                g[j, part, i // 4, i % 4] = half.reshape(4, 48, CH)

        direct_start(j)

        for h in (0, 16):

            def tap_terms(i, total):
                u, b = i // 4, i % 4
                window = xe[u, pl.ds(b * 8 + h, 23)]
                grads = de[u, pl.ds(16 + b * 8, 8)]
                for m in range(8):
                    total = total + grads[m][None] * window[m : m + 16]
                return total

            terms = lax.fori_loop(0, 8, tap_terms, jnp.zeros((16, 8, CH), F32), unroll=4)
            tg[j, h : h + 16] = jnp.sum(terms, axis=1)
        for u in (0, 1):
            rows = slice(u * ROWS, (u + 1) * ROWS)
            dpn[j, rows, :] = dot(from_phase, dp[rows, :]).astype(BF16)

        @pl.when(j >= 1)
        def _():
            direct_finish(j - 1)

        @pl.when(j >= 2)
        def _():
            stage2_finish(j - 2)

        @pl.when(jnp.logical_and(j >= 3, j % 2 == 1))
        def _():
            stage3_start((j - 3) // 2, 512)

        return 0

    lax.fori_loop(0, NC, chunk, 0)

    for j in range(NC):
        tt[j * CH : (j + 1) * CH, :] = tg[j].T.astype(BF16)
    for d in (1, 2, 3):
        send(tt.at[pl.ds(pl.multiple_of(zd(d) * 192, 16), 192)], t_r1.at[d - 1],
             t_send.at[0], t_recv.at[0], dev(c, zd(d), y, x))

    dims = (((1,), (1,)), ((), ()))

    def dnormed(u, cols):
        rows = pl.ds(pl.multiple_of(u * ROWS, ROWS), ROWS)
        total = dot(dpn[0, rows, :], w_vm[0, cols, :], dims)
        for j in range(1, NC):
            total = total + dot(dpn[j, rows, :], w_vm[j, cols, :], dims)
        return total

    def sibling_part(i, _):
        cols = pl.ds(pl.multiple_of(i * 256, 256), 256)
        dns[:, cols] = dnormed(oc, cols).astype(BF16)
        return 0

    lax.fori_loop(0, D // 256, sibling_part, 0)
    send(dns, dnr, misc_send.at[6], misc_recv.at[6], sibling)

    direct_finish(NC - 1)
    stage2_finish(NC - 2)
    await_bytes(t_r1, t_recv.at[0])
    mine = tt[pl.ds(pl.multiple_of(z * 192, 16), 192), :].astype(F32)
    for d in range(3):
        mine = mine + t_r1[d].astype(F32)
    t_s1[...] = mine.astype(BF16)
    for d in (1, 2, 3):
        send(t_s1.at[pl.ds(pl.multiple_of(yd(d) * 48, 16), 48)], t_r2.at[d - 1],
             t_send.at[1], t_recv.at[1], dev(c, z, yd(d), x))

    def own_part(i, _):
        cols = pl.ds(pl.multiple_of(i * 256, 256), 256)
        dno[:, cols] = dnormed(c, cols)
        return 0

    lax.fori_loop(0, D // 256, own_part, 0)

    stage2_finish(NC - 1)
    await_bytes(t_r2, t_recv.at[1])
    mine = t_s1[pl.ds(pl.multiple_of(y * 48, 16), 48), :].astype(F32)
    for d in range(3):
        mine = mine + t_r2[d].astype(F32)
    sf[0, 0:48] = mine
    for b in range(4):
        fs[2, c, b, :, 512:640] = sf[0, 12 * b : 12 * b + 16].astype(BF16)

    stage3_start(2, 640)

    await_bytes(dnr, misc_recv.at[6])

    def input_rows(i, _):
        rows = pl.ds(pl.multiple_of(i * 32, 32), 32)
        average, inverse = stat[0, rows, 0:1], stat[1, rows, 0:1]
        xhat = (x_vm[rows, :].astype(F32) - average) * inverse
        grad = dno[rows, :] + dnr[rows, :].astype(F32)
        m1 = jnp.mean(grad, axis=-1, keepdims=True)
        m2 = jnp.mean(grad * xhat, axis=-1, keepdims=True)
        gx_vm[rows, :] = (inverse * (grad - m1 - xhat * m2)).astype(BF16)
        return 0

    lax.fori_loop(0, ROWS // 32, input_rows, 0)
    store_gx = pltpu.make_async_copy(gx_vm, gx_hbm.at[0], local_sem.at[0])
    store_gx.start()

    squares = stage3_finish(0, 512) + stage3_finish(1, 512) + stage3_finish(2, 640)
    total = r3[2, 0, 0, :, 512:640].astype(F32)
    for d in range(1, 4):
        total = total + r3[2, 0, d, :, 512:640].astype(F32)
    tap_rows = total[0:12]
    squares = squares + tap_rows * tap_rows

    part = jnp.sum(jnp.sum(squares, axis=0, keepdims=True), axis=1, keepdims=True)
    ps_s[0] = jnp.broadcast_to(part, (8, 128))
    count = 0
    for e in (0, 1):
        for d in range(4):
            if e == 0 and d == 0:
                continue
            send(ps_s.at[0], ps_r.at[count], ps_send.at[0], ps_recv.at[0],
                 dev(c if e == 0 else oc, z, y, xd(d)))
            count += 1
    await_bytes(ps_r.at[0:7], ps_recv.at[0])
    total = ps_s[0]
    for i in range(7):
        total = total + ps_r[i]
    ps_s[1] = total
    count = 7
    for d in range(4):
        for e in range(4):
            if d == 0 and e == 0:
                continue
            send(ps_s.at[1], ps_r.at[count], ps_send.at[1], ps_recv.at[1], dev(c, zd(d), yd(e), x))
            count += 1
    await_bytes(ps_r.at[7:22], ps_recv.at[1])
    total = ps_s[1]
    for i in range(7, 22):
        total = total + ps_r[i]
    msq = total[0:1, 0:1] / jnp.float32(2 * D * D + D * KT)
    scale = 1.0 / jnp.maximum(jnp.float32(1.0), jnp.sqrt(msq))
    gin_vm[...] = gin_vm[...] * scale
    gtap_vm[...] = (tap_rows * scale)[:, 0:KT]
    store_gin = pltpu.make_async_copy(gin_vm, gin_hbm, local_sem.at[1])
    store_gin.start()
    store_gtap = pltpu.make_async_copy(gtap_vm, gtap_hbm, local_sem.at[2])
    store_gtap.start()

    for j in range(NC):
        await_bytes(w_vm.at[j, pl.ds(0, H)], w_send.at[j])
        for part in (0, 1):
            await_bytes(r2.at[j, part], r2_send.at[j, part])
    for j in range(NC):
        for part in (0, 1):
            await_bytes(rd.at[j, part], rd_send.at[j, part])
    await_bytes(cot_sib, misc_send.at[0])
    await_bytes(cot_halo, misc_send.at[1])
    await_bytes(tap_in, misc_send.at[2])
    await_bytes(edges, misc_send.at[3])
    await_bytes(na.at[own_rows], misc_send.at[4])
    await_bytes(halo.at[c], misc_send.at[5])
    await_bytes(dns, misc_send.at[6])
    await_bytes(fb_r.at[0, 0:3], fb_send.at[0])
    await_bytes(fb_r.at[1], fb_send.at[1])
    for q, width in ((0, 512), (1, 512), (2, 640)):
        stage3_await(q, width, r3_send)
    await_bytes(t_r1, t_send.at[0])
    await_bytes(t_r2, t_send.at[1])
    await_bytes(ps_r.at[0:7], ps_send.at[0])
    await_bytes(ps_r.at[7:22], ps_send.at[1])
    store_gx.wait()
    store_gin.wait()
    store_gtap.wait()


def hand_over(gx, gin, gtap, gx_out, gin_out, gtap_out):
    gx_out[...] = gx[...]
    gin_out[...] = gin[...]
    gtap_out[...] = gtap[...]


def body(activations, cotangent, lengths, poison, w_in, taps):
    vmem = pltpu.VMEM
    dma = pltpu.SemaphoreType.DMA
    scratch = [
        vmem((ROWS, D), BF16),
        vmem((ROWS, D), BF16),
        vmem((ROWS, H), BF16),
        vmem((2, 2, 16, H), BF16),
        vmem((2, 32, D), BF16),
        vmem((ROWS, D), BF16),
        vmem((2, 2, 32, D), BF16),
        vmem((640, D), BF16),
        vmem((D, 512), BF16),
        vmem((NC, D, 2 * CH), BF16),
        vmem((2, ROWS, H), BF16),
        vmem((128, H), BF16),
        vmem((KT, H), BF16),
        vmem((KT, H), F32),
        vmem((KT, 8, CH), F32),
        vmem((640, 128), F32),
        vmem((640, 128), F32),
        vmem((2, ROWS, 128), F32),
        vmem((640, 2 * CH), F32),
        vmem((512, CH), F32),
        vmem((512, CH), F32),
        vmem((2, 64, 8, CH), F32),
        vmem((48, 8, CH), F32),
        vmem((2, 64, 8, CH), F32),
        vmem((16, 8, CH), F32),
        vmem((512, 2 * CH), BF16),
        vmem((NC, 512, 2 * CH), BF16),
        vmem((NC, 128, CH), F32),
        vmem((H, 128), BF16),
        vmem((NC, 2, 2, 4, 4, 48, CH), BF16),
        vmem((NC, 2, 3, 2, 4, 48, CH), BF16),
        vmem((NC, 2, 2, 4, 48, CH), BF16),
        vmem((NC, 2, 3, 2, 48, CH), BF16),
        vmem((3, 2, 4, 16, 640), BF16),
        vmem((3, 2, 4, 16, 640), BF16),
        vmem((2, 56, CH), F32),
        vmem((3, 192, 128), BF16),
        vmem((192, 128), BF16),
        vmem((3, 48, 128), BF16),
        vmem((ROWS, D), F32),
        vmem((ROWS, D), BF16),
        vmem((ROWS, D), BF16),
        vmem((ROWS, D), BF16),
        vmem((12, 2 * D), F32),
        vmem((12, KT), F32),
        vmem((2, 8, 128), jnp.int32),
        vmem((2, 15, 8, 128), jnp.int32),
        vmem((2, 8, 128), F32),
        vmem((22, 8, 128), F32),
        dma((3,)),
        dma((NC,)), dma((NC,)), dma((NC, 2)),
        dma((7,)), dma((7,)),
        dma((2,)), dma((2,)),
        dma((NC, 2)), dma((NC, 2)),
        dma((NC, 2)), dma((NC, 2)),
        dma((3, 2)), dma((3, 2)),
        dma((2,)), dma((2,)),
        dma((2,)), dma((2,)),
    ]
    anywhere = pl.BlockSpec(memory_space=pl.ANY)
    in_vmem = pl.BlockSpec(memory_space=pltpu.VMEM)
    in_smem = pl.BlockSpec(memory_space=pltpu.SMEM)
    shapes = (
        jax.ShapeDtypeStruct((1, ROWS, D), BF16),
        jax.ShapeDtypeStruct((12, 2 * D), F32),
        jax.ShapeDtypeStruct((12, KT), F32),
    )
    results = pl.pallas_call(
        kernel,
        out_shape=shapes,
        in_specs=[in_smem, in_smem, in_vmem, anywhere, anywhere, anywhere],
        out_specs=(anywhere, anywhere, anywhere),
        scratch_shapes=scratch,
        compiler_params=pltpu.CompilerParams(
            collective_id=0, has_side_effects=True, vmem_limit_bytes=56 * 1024 * 1024
        ),
        name="conformer_conv",
    )(lengths, poison, taps.T, activations, cotangent, w_in)
    return pl.pallas_call(
        hand_over,
        out_shape=shapes,
        in_specs=[in_vmem] * 3,
        out_specs=(in_vmem,) * 3,
        name="hand_over",
    )(*results)


def solution(mesh):
    placed = (
        P(("dp", "fsdp"), "seq", None),
        P(("dp", "fsdp"), "seq", None),
        P(("dp", "fsdp")),
        P(("dp", "fsdp"), "seq"),
        P("fsdp", None),
        P("fsdp", None),
    )
    return jax.shard_map(
        body,
        mesh=mesh,
        in_specs=placed,
        out_specs=(
            P(("dp", "fsdp"), "seq", None),
            P(("dp", "seq", "fsdp"), None),
            P(("dp", "seq", "fsdp"), None),
        ),
        check_vma=False,
    )
```
